256 devices in a mesh: section: 8 (over z), feat: 32 (over x, y, core).
Axes of the slice: x: 4, y: 4, z: 8, core: 2. Of those that a mesh axis runs over, the one named last changes fastest.
Arguments:
- inputs: bfloat16 [8, 512, 2560], P('section', 'feat'), may hold values from -6 to 6
- enc_weight: bfloat16 [8, 2560, 4096], P('section', None, 'feat'), may hold values from -0.125 to 0.125
- enc_bias: float32 [8, 4096], P('section', 'feat'), may hold values from -3 to 3
- dec_weight: bfloat16 [8, 8, 4096, 2560], P('section', None, 'feat'), may hold values from -0.09375 to 0.09375
- dec_bias: bfloat16 [8, 2560], P('section'), may hold values from -3 to 3
- target: bfloat16 [8, 512, 2560], P('section', 'feat'), may hold values from -6 to 6
- active: int32 [8, 16, 8], P('section'), may hold values from 0 to 31, all different within a row
Outputs:
- enc_grad: bfloat16 [8, 2560, 4096], P('section', None, 'feat')
- bias_grad: float32 [8, 4096], P('section', 'feat')
- dec_grad: bfloat16 [8, 8, 4096, 2560], P('section', None, 'feat')
The draws below stay inside these ranges and needn't reach their ends.
Inputs may be any that keep to these rules, and one draw needn't show every extreme that they name: `active`: each row names 8 different blocks of 32; every block is named by some row.
All inputs are finite; a program needn't handle non-finite values.
Results may differ from the reference program's by a relative error of at most 0.024.
Values may be sent and summed in bfloat16 or wider, within the bound.
A program may use at most 128 MiB of HBM per device.

```python
import jax
import jax.numpy as jnp
from jax import lax

D = 2560
F = 4096
FBLK = 128
K = 8
TBLK = 32
TOKENS = 512
LAYERS = 8
NB = 32
NTB = 16


def level_of(key, extent, pieces, least, high):
    def one(dim, shards_of):
        steps = jax.random.uniform(jax.random.fold_in(jax.random.fold_in(key, 6), dim), (shards_of,), jnp.float32, least / len(pieces), high / len(pieces))
        return jnp.repeat(jnp.exp(steps), extent[dim] // shards_of).reshape((-1,) + (1,) * (len(extent) - dim - 1))

    loudness = one(*pieces[0])
    for cut in pieces[1:]:
        loudness = loudness * one(*cut)
    return loudness


def picks_of(key, rows, number_of, top, lift):
    sequence = jax.random.permutation(jax.random.fold_in(key, 1), number_of)
    boost = sequence
    for power in range(3):
        boost = boost * boost // number_of
    boost = boost * lift // number_of
    tickets = jax.random.randint(jax.random.fold_in(key, 2), (rows, number_of), 0, 4096) + boost
    sure = jax.random.permutation(jax.random.fold_in(key, 3), rows)[jnp.arange(number_of) % rows]
    tickets = jnp.where(jnp.arange(rows)[:, None] == sure[None, :], 1 << 14, tickets)
    priority = tickets * number_of + jnp.arange(number_of)
    return lax.top_k(priority.astype(jnp.int32), top)[1].astype(jnp.int32)


def bell_draw(own_key, dims, spread, reach, pieces=(), kind=jnp.bfloat16):
    array = spread * jax.random.normal(own_key, dims, jnp.float32)
    if pieces:
        array = array * level_of(own_key, dims, pieces, -0.22, 0.18)
    return jnp.clip(array, -reach, reach).astype(kind)


def setup_inputs(seed: int = 0) -> dict:
    key_of = jax.random.split(jax.random.key(seed), 8)
    inputs = bell_draw(key_of[0], (LAYERS, TOKENS, D), 1.0, 6.0, ((0, 8), (1, 32)))
    enc_weight = bell_draw(key_of[1], (LAYERS, D, F), D ** -0.5, 0.125, ((0, 8), (2, 32)))
    enc_bias = bell_draw(key_of[2], (LAYERS, F), 0.5, 3.0, ((0, 8), (1, 32)), jnp.float32)
    dec_weight = bell_draw(key_of[3], (LAYERS, LAYERS, F, D), F ** -0.5, 0.09375, ((0, 8), (2, 32)))
    dec_bias = bell_draw(key_of[4], (LAYERS, D), 0.5, 3.0, ((0, 8),))
    target = bell_draw(key_of[5], (LAYERS, TOKENS, D), 1.0, 6.0, ((0, 8), (1, 32)))
    active = picks_of(key_of[6], LAYERS * NTB, NB, K, 4096).reshape((LAYERS, NTB, K))
    return dict(inputs=inputs, enc_weight=enc_weight, enc_bias=enc_bias, dec_weight=dec_weight, dec_bias=dec_bias, target=target, active=active)


def reference(inputs, enc_weight, enc_bias, dec_weight, dec_bias, target, active):
    block_ids = lax.iota(jnp.int32, F) // FBLK
    live_list = []
    code_list = []
    for layer in range(LAYERS):
        pre_act = jnp.dot(inputs[layer], enc_weight[layer], preferred_element_type=jnp.float32) + enc_bias[layer][None, :]
        matched = jnp.any(active[layer][:, :, None] == block_ids[None, None, :], axis=1)
        keep_mask = jnp.repeat(matched.astype(jnp.float32), TBLK, axis=0)
        live_mask = keep_mask * (pre_act > 0).astype(jnp.float32)
        live_list.append(live_mask)
        code_list.append((live_mask * pre_act).astype(jnp.bfloat16))
    code_grad = [jnp.zeros((TOKENS, F), jnp.float32) for layer in range(LAYERS)]
    dec_rows = []
    for target_layer in range(LAYERS):
        rebuilt = jnp.zeros((TOKENS, D), jnp.float32)
        for source in range(target_layer + 1):
            rebuilt = rebuilt + jnp.dot(code_list[source], dec_weight[target_layer, source], preferred_element_type=jnp.float32)
        residual = (rebuilt + dec_bias[target_layer].astype(jnp.float32)[None, :] - target[target_layer].astype(jnp.float32)).astype(jnp.bfloat16)
        blocks = []
        for source in range(LAYERS):
            if source <= target_layer:
                blocks.append(jnp.dot(code_list[source].T, residual, preferred_element_type=jnp.float32).astype(jnp.bfloat16))
                code_grad[source] = code_grad[source] + jnp.dot(residual, dec_weight[target_layer, source].T, preferred_element_type=jnp.float32)
            else:
                blocks.append(jnp.zeros((F, D), jnp.bfloat16))
        dec_rows.append(jnp.stack(blocks))
    enc_list = []
    bias_list = []
    for layer in range(LAYERS):
        pre_grad = (code_grad[layer] * live_list[layer]).astype(jnp.bfloat16)
        enc_list.append(jnp.dot(inputs[layer].T, pre_grad, preferred_element_type=jnp.float32).astype(jnp.bfloat16))
        bias_list.append(jnp.sum(pre_grad.astype(jnp.float32), axis=0))
    return jnp.stack(enc_list), jnp.stack(bias_list), jnp.stack(dec_rows)
```

```python
import functools

import jax
import jax.numpy as jnp
from jax import lax
from jax.experimental import pallas as pl
from jax.experimental.pallas import tpu as pltpu
from jax.sharding import PartitionSpec as P

MESH = pl.DeviceIdType.MESH
BF16 = jnp.bfloat16
F32 = jnp.float32

NX = 4
NY = 4
CHIPS = NX * NY
NZ = 8
ROWS = 16
FW = 128
D = 2560
TOK = CHIPS * ROWS
PAIR = 2 * FW
HALF = TOK // 2
TILE = 512

PLANE = [(dx, dy) for dx in range(NX) for dy in range(NY) if (dx, dy) != (0, 0)]
PLANE.sort(key=lambda o: -(min(o[0], NX - o[0]) + min(o[1], NY - o[1])))


def step_kernel(
    x_ref, we_ref, be_ref, wd_ref, bd_ref, tg_ref, act_ref,
    xo_ref, ro_ref, co_ref, pg_ref,
    xg, rg, we_s, wd_s, be_s, be_t, vis, live, acc, rb, rsr, cs, pg_s, zsb, zrb,
    in_sem, in_ssem, in_rsem, a_ssem, a_rsem, b_ssem, b_rsem, c_ssem, c_rsem,
    e_ssem, e_rsem, g_ssem, g_rsem, p_ssem, p_rsem, out_sem,
):
    s = lax.axis_index("section")
    f = lax.axis_index("feat")
    core = lax.rem(f, 2)
    chip = lax.div(f, 2)
    cx = lax.div(chip, NY)
    cy = lax.rem(chip, NY)

    def plane_chip(o):
        return lax.rem(cx + o[0], NX) * NY + lax.rem(cy + o[1], NY)

    def plane_dev(o):
        return {"section": s, "feat": plane_chip(o) * 2 + core}

    peer = {"section": s, "feat": chip * 2 + 1 - core}
    up = {"section": lax.rem(s + 1, NZ), "feat": f}
    down = {"section": lax.rem(s + NZ - 1, NZ), "feat": f}

    def remote(src, dst, ssem, rsem, dev):
        return pltpu.make_async_remote_copy(
            src_ref=src, dst_ref=dst, send_sem=ssem, recv_sem=rsem, device_id=dev, device_id_type=MESH
        )

    barrier = pltpu.get_barrier_semaphore()
    for dev in [peer, up, down] + [plane_dev(o) for o in PLANE]:
        pl.semaphore_signal(barrier, inc=1, device_id=dev, device_id_type=MESH)

    loc = [pltpu.make_async_copy(we_ref, we_s.at[:, pl.ds(0, FW)], in_sem.at[NZ])]
    for l in range(NZ):
        loc.append(pltpu.make_async_copy(wd_ref.at[l], wd_s.at[l, pl.ds(0, FW)], in_sem.at[l]))
    for cp in loc:
        cp.start()
    be_t[...] = jnp.broadcast_to(be_ref[...], (8, FW))
    xg[0, chip] = x_ref[...]

    pl.semaphore_wait(barrier, 3 + len(PLANE))

    ag_x = [
        remote(x_ref, xg.at[0, chip], a_ssem.at[k], a_rsem.at[k], plane_dev(o)) for k, o in enumerate(PLANE)
    ]
    for cp in ag_x:
        cp.start()
    swap = [
        remote(we_ref, we_s.at[:, pl.ds(FW, FW)], in_ssem.at[NZ], in_rsem.at[NZ], peer),
        remote(be_t, be_s, in_ssem.at[NZ + 1], in_rsem.at[NZ + 1], peer),
    ]
    for l in range(NZ):
        swap.append(remote(wd_ref.at[l], wd_s.at[l, pl.ds(FW, FW)], in_ssem.at[l], in_rsem.at[l], peer))
    for cp in swap:
        cp.start()

    act = act_ref[...]
    row_chip = lax.broadcasted_iota(jnp.int32, (TOK, CHIPS), 0) // ROWS
    expand = (row_chip == lax.broadcasted_iota(jnp.int32, (TOK, CHIPS), 1)).astype(F32)

    def keep_of(block):
        hit = jnp.max((act == block).astype(F32), axis=1, keepdims=True)
        return jnp.dot(expand, jnp.broadcast_to(hit, (CHIPS, FW)), preferred_element_type=F32)

    live[:, 0:FW] = keep_of(f)
    live[:, FW:PAIR] = keep_of(chip * 2 + 1 - core)

    loc[0].wait()
    swap[0].wait_recv()
    swap[1].wait_recv()
    for cp in ag_x:
        cp.wait_recv()

    pre = jnp.dot(xg[0].reshape(TOK, D), we_s[...], preferred_element_type=F32)
    bias = jnp.concatenate([be_t[0:1, :], be_s[0:1, :]], axis=1)
    pre = pre + bias
    mask = live[...] * (pre > 0).astype(F32)
    live[...] = mask
    vis[s] = (mask * pre).astype(BF16)

    def zcopy(way, hop, half):
        block = lax.rem(s - hop + 1 + NZ, NZ) if way == 0 else lax.rem(s + hop - 1, NZ)
        ref = vis.at[block, pl.ds(half * HALF, HALF)]
        return remote(ref, ref, b_ssem.at[way, hop - 1, half], b_rsem.at[way, hop - 1, half], up if way == 0 else down)

    def zhalves(way, hop):
        return (0, 1) if hop < 4 else (way,)

    zsends = {}
    for half in (0, 1):
        for way in (0, 1):
            cp = zcopy(way, 1, half)
            cp.start()
            zsends[way, 1, half] = cp

    swap_x = remote(xg.at[0], xg.at[1], p_ssem.at[0], p_rsem.at[0], peer)
    swap_x.start()

    for l in range(NZ):
        loc[1 + l].wait()
        swap[2 + l].wait_recv()

    def add_block(block, first=False):
        @pl.loop(0, D // TILE)
        def _(j):
            col = pl.ds(pl.multiple_of(j * TILE, TILE), TILE)
            part = jnp.dot(vis[block], wd_s[block, :, col], preferred_element_type=F32)
            if first:
                acc[:, col] = part
            else:
                acc[:, col] += part

    add_block(s, True)
    for hop in (1, 2, 3):
        for half in (0, 1):
            for way in (0, 1):
                zsends[way, hop, half].wait_recv()
                if half in zhalves(way, hop + 1):
                    cp = zcopy(way, hop + 1, half)
                    cp.start()
                    zsends[way, hop + 1, half] = cp

        @pl.when(s >= hop)
        def _():
            add_block(lax.rem(s - hop + NZ, NZ))

        @pl.when(s + hop >= NZ)
        def _():
            add_block(lax.rem(s + hop, NZ))

    for way in (0, 1):
        zsends[way, 4, way].wait_recv()

    @pl.when(s >= 4)
    def _():
        add_block(lax.rem(s + 4, NZ))

    for i in range(CHIPS):
        rb[i] = acc[i * ROWS:(i + 1) * ROWS, :].astype(BF16)
    rs = [
        remote(rb.at[plane_chip(o)], rsr.at[chip], c_ssem.at[k], c_rsem.at[k], plane_dev(o))
        for k, o in enumerate(PLANE)
    ]
    for cp in rs:
        cp.start()
    swap_c = remote(vis.at[:, :, pl.ds(FW, FW)], cs.at[:, 1], p_ssem.at[1], p_rsem.at[1], peer)
    swap_c.start()
    total = acc[pl.ds(pl.multiple_of(chip * ROWS, ROWS), ROWS), :] + bd_ref[...].astype(F32) - tg_ref[...].astype(F32)
    cs[:, 0] = vis[:, :, 0:FW]
    for k, o in enumerate(PLANE):
        rs[k].wait_recv()
        src = lax.rem(cx + NX - o[0], NX) * NY + lax.rem(cy + NY - o[1], NY)
        total = total + rsr[src].astype(F32)
    rg[0, chip] = total.astype(BF16)

    ag_r = [
        remote(rg.at[0, chip], rg.at[0, chip], e_ssem.at[k], e_rsem.at[k], plane_dev(o)) for k, o in enumerate(PLANE)
    ]
    for cp in ag_r:
        cp.start()
    swap_x.wait_recv()
    out_x = pltpu.make_async_copy(xg, xo_ref, out_sem.at[0])
    out_x.start()
    swap_c.wait_recv()
    out_c = pltpu.make_async_copy(cs, co_ref, out_sem.at[1])
    out_c.start()
    for cp in ag_r:
        cp.wait_recv()
    swap_r = remote(rg.at[0], rg.at[1], p_ssem.at[2], p_rsem.at[2], peer)
    swap_r.start()

    def code_grad(block):
        return lax.dot_general(
            rg[0].reshape(TOK, D), wd_s[block], (((1,), (1,)), ((), ())), preferred_element_type=F32
        )

    def gcopy(way, j, half):
        return remote(
            zsb.at[way, j - 1, half], zrb.at[way, j - 1, half],
            g_ssem.at[way, j - 1, half], g_rsem.at[way, j - 1, half], down if way == 0 else up,
        )

    gsends = {}
    for j in (4, 3, 2, 1):
        for way in (0, 1):
            if way == 0:
                block, given = lax.rem(s - j + NZ, NZ), s >= j
            else:
                block, given = lax.rem(s + j, NZ), s + j >= NZ
            if j == 4:
                if way == 0:
                    acc[:, 0:PAIR] = jnp.where(given, code_grad(block), 0.0)
                part = acc[way * HALF:(way + 1) * HALF, 0:PAIR]
                parts = {way: part}
            else:
                acc[:, 0:PAIR] = jnp.where(given, code_grad(block), 0.0)
                parts = {h: acc[h * HALF:(h + 1) * HALF, 0:PAIR] for h in (way, 1 - way)}
            for half, part in parts.items():
                if (way, j + 1, half) in gsends:
                    gsends[way, j + 1, half].wait_recv()
                    part = part + zrb[way, j, half].astype(F32)
                zsb[way, j - 1, half] = part.astype(BF16)
                cp = gcopy(way, j, half)
                cp.start()
                gsends[way, j, half] = cp

    acc[:, 0:PAIR] = code_grad(s)
    swap_r.wait_recv()
    out_r = pltpu.make_async_copy(rg, ro_ref, out_sem.at[2])
    out_r.start()
    for half in (0, 1):
        rows = slice(half * HALF, (half + 1) * HALF)
        own = acc[rows, 0:PAIR]
        for way in (0, 1):
            gsends[way, 1, half].wait_recv()
            own = own + zrb[way, 0, half].astype(F32)
        grad = (own * live[rows, :]).astype(BF16)
        pg_s[0, 0, rows, :] = grad[:, 0:FW]
        pg_s[1, 0, rows, :] = grad[:, FW:PAIR]
    swap_g = remote(pg_s.at[1, 0], pg_s.at[0, 1], p_ssem.at[3], p_rsem.at[3], peer)
    swap_g.start()
    swap_g.wait_recv()
    pg_ref[...] = pg_s[0]

    for cp in ag_x + ag_r + rs + swap + [swap_x, swap_c, swap_r, swap_g]:
        cp.wait_send()
    for cp in list(zsends.values()) + list(gsends.values()):
        cp.wait_send()
    out_x.wait()
    out_c.wait()
    out_r.wait()


def fused(x, we, be, wd, bd, tg, act):
    vmem = pl.BlockSpec(memory_space=pltpu.VMEM)
    hbm = pl.BlockSpec(memory_space=pl.ANY)
    dma = pltpu.SemaphoreType.DMA
    n = len(PLANE)
    return pl.pallas_call(
        step_kernel,
        name="step",
        out_shape=(
            jax.ShapeDtypeStruct((2, CHIPS, ROWS, D), BF16),
            jax.ShapeDtypeStruct((2, CHIPS, ROWS, D), BF16),
            jax.ShapeDtypeStruct((NZ, 2, TOK, FW), BF16),
            jax.ShapeDtypeStruct((2, TOK, FW), BF16),
        ),
        in_specs=[vmem, hbm, vmem, hbm, vmem, vmem, vmem],
        out_specs=(hbm, hbm, hbm, vmem),
        scratch_shapes=[
            pltpu.VMEM((2, CHIPS, ROWS, D), BF16),
            pltpu.VMEM((2, CHIPS, ROWS, D), BF16),
            pltpu.VMEM((D, PAIR), BF16),
            pltpu.VMEM((NZ, PAIR, D), BF16),
            pltpu.VMEM((8, FW), F32),
            pltpu.VMEM((8, FW), F32),
            pltpu.VMEM((NZ, TOK, PAIR), BF16),
            pltpu.VMEM((TOK, PAIR), F32),
            pltpu.VMEM((TOK, D), F32),
            pltpu.VMEM((CHIPS, ROWS, D), BF16),
            pltpu.VMEM((CHIPS, ROWS, D), BF16),
            pltpu.VMEM((NZ, 2, TOK, FW), BF16),
            pltpu.VMEM((2, 2, TOK, FW), BF16),
            pltpu.VMEM((2, 4, 2, HALF, PAIR), BF16),
            pltpu.VMEM((2, 4, 2, HALF, PAIR), BF16),
            dma((NZ + 1,)), dma((NZ + 2,)), dma((NZ + 2,)),
            dma((n,)), dma((n,)),
            dma((2, 4, 2)), dma((2, 4, 2)),
            dma((n,)), dma((n,)),
            dma((n,)), dma((n,)),
            dma((2, 4, 2)), dma((2, 4, 2)),
            dma((4,)), dma((4,)),
            dma((3,)),
        ],
        compiler_params=pltpu.CompilerParams(
            collective_id=0, has_side_effects=True, vmem_limit_bytes=56 * 2**20
        ),
    )(x, we, be, wd, bd, tg, act)


def body(inputs, enc_weight, enc_bias, dec_weight, dec_bias, target, active):
    xa, ra, codes, pg = fused(
        inputs[0], enc_weight[0], enc_bias, dec_weight[0], dec_bias, target[0], active[0]
    )
    xa = xa.reshape(2 * TOK, D)
    ra = ra.reshape(2 * TOK, D)
    codes = codes.reshape(NZ, 2 * TOK, FW)
    pg = pg.reshape(2 * TOK, FW)
    causal = (lax.iota(jnp.int32, NZ) <= lax.axis_index("section")).astype(BF16)
    codes = codes * causal[:, None, None]
    enc_grad = jnp.einsum("td,tf->df", xa, pg, preferred_element_type=F32).astype(BF16)
    bias_grad = jnp.sum(pg.astype(F32), axis=0)
    dec_grad = jnp.einsum("ltf,td->lfd", codes, ra, preferred_element_type=F32).astype(BF16)
    return enc_grad[None], bias_grad[None], dec_grad[None]


def solution(mesh):
    return jax.shard_map(
        body,
        mesh=mesh,
        in_specs=(
            P("section", "feat", None),
            P("section", None, "feat"),
            P("section", "feat"),
            P("section", None, "feat", None),
            P("section", None),
            P("section", "feat", None),
            P("section", None, None),
        ),
        out_specs=(
            P("section", None, "feat"),
            P("section", "feat"),
            P("section", None, "feat", None),
        ),
        check_vma=False,
    )
```

```python
import functools

import jax
import jax.numpy as jnp
from jax import lax
from jax.experimental import pallas as pl
from jax.experimental.pallas import tpu as pltpu
from jax.sharding import PartitionSpec as P

MESH = pl.DeviceIdType.MESH
BF16 = jnp.bfloat16
F32 = jnp.float32

NX = 4
NY = 4
CHIPS = NX * NY
NZ = 8
ROWS = 16
FW = 128
D = 2560
TOK = CHIPS * ROWS
PAIR = 2 * FW
HALF = TOK // 2
TILE = 512

HD = D // 2
LEFT = pl.ds(0, HD)
RIGHT = pl.ds(HD, HD)


def step_kernel(
    x_ref, we_ref, be_ref, wd_ref, bd_ref, tg_ref, act_ref,
    eg_ref, bg_ref, dg_ref,
    xg, rg, we_s, wd_s, be_s, bd_s, tg_s, act_s, vis, live, acc, rb, r1, r2s, r2, tot, cs, ct, xt, pg_s, zsb, zrb,
    in_sem, in_ssem, in_rsem, a_ssem, a_rsem, b_ssem, b_rsem, c_ssem, c_rsem,
    e_ssem, e_rsem, g_ssem, g_rsem, p_ssem, p_rsem, small_sem,
):
    s = lax.axis_index("section")
    f = lax.axis_index("feat")
    core = lax.rem(f, 2)
    chip = lax.div(f, 2)
    cx = lax.div(chip, NY)
    cy = lax.rem(chip, NY)

    def along(axis, step):
        x = lax.rem(cx + step, NX) if axis == 0 else cx
        y = lax.rem(cy + step, NY) if axis == 1 else cy
        return {"section": s, "feat": (x * NY + y) * 2 + core}

    peer = {"section": s, "feat": chip * 2 + 1 - core}
    up = {"section": lax.rem(s + 1, NZ), "feat": f}
    down = {"section": lax.rem(s + NZ - 1, NZ), "feat": f}
    up2 = {"section": lax.rem(s + 2, NZ), "feat": f}
    down2 = {"section": lax.rem(s + NZ - 2, NZ), "feat": f}

    def remote(src, dst, ssem, rsem, dev):
        return pltpu.make_async_remote_copy(
            src_ref=src, dst_ref=dst, send_sem=ssem, recv_sem=rsem, device_id=dev, device_id_type=MESH
        )

    barrier = pltpu.get_barrier_semaphore()
    for dev in [peer, up, down, up2, down2] + [along(axis, o) for axis in (0, 1) for o in (1, 2, 3)]:
        pl.semaphore_signal(barrier, inc=1, device_id=dev, device_id_type=MESH)

    loc = [pltpu.make_async_copy(we_ref, we_s.at[:, pl.ds(0, FW)], in_sem.at[NZ])]
    for l in range(NZ):
        loc.append(pltpu.make_async_copy(wd_ref.at[l], wd_s.at[l, pl.ds(0, FW)], in_sem.at[l]))
    small = [
        pltpu.make_async_copy(a, b, small_sem.at[k])
        for k, (a, b) in enumerate(
            [(act_ref, act_s), (be_ref, be_s.at[0]), (x_ref, xg.at[0, 0, 0]), (bd_ref, bd_s), (tg_ref, tg_s)]
        )
    ]
    for cp in small + loc:
        cp.start()

    pl.semaphore_wait(barrier, 11)

    def gather_first(src, g, ssem, rsem):
        copies = {}
        for o in (2, 1, 3):
            for axis in (0, 1):
                there = (NX - o, 0) if axis == 0 else (0, NY - o)
                cp = remote(src, g.at[0, there[0], there[1]], ssem.at[0, axis, o - 1], rsem.at[0, axis, o - 1], along(axis, o))
                cp.start()
                copies[axis, o] = cp
        return copies

    def gather_second(first, g, ssem, rsem):
        copies = []
        for axis in (0, 1):
            for o in (1, 3, 2):
                first[axis, o].wait_recv()
            for o in (2, 1, 3):
                if axis == 0:
                    src, dst = g.at[0, pl.ds(1, 3), 0, :, LEFT], g.at[0, pl.ds(1, 3), NY - o, :, LEFT]
                else:
                    src, dst = g.at[0, 0, pl.ds(1, 3), :, RIGHT], g.at[0, NX - o, pl.ds(1, 3), :, RIGHT]
                cp = remote(src, dst, ssem.at[1, axis, o - 1], rsem.at[1, axis, o - 1], along(1 - axis, o))
                cp.start()
                copies.append(cp)
        return copies

    ag_x1 = gather_first(x_ref, xg, a_ssem, a_rsem)
    swap = [
        remote(we_ref, we_s.at[:, pl.ds(FW, FW)], in_ssem.at[NZ], in_rsem.at[NZ], peer),
        remote(be_ref, be_s.at[1], in_ssem.at[NZ + 1], in_rsem.at[NZ + 1], peer),
    ]
    for l in range(NZ):
        swap.append(remote(wd_ref.at[l], wd_s.at[l, pl.ds(FW, FW)], in_ssem.at[l], in_rsem.at[l], peer))
    for cp in swap:
        cp.start()

    small[0].wait()
    act = act_s[...]
    row_at = lax.broadcasted_iota(jnp.int32, (TOK, CHIPS), 0) // ROWS
    row_chip = lax.rem(cx + row_at // NY, NX) * NY + lax.rem(cy + lax.rem(row_at, NY), NY)
    expand = (row_chip == lax.broadcasted_iota(jnp.int32, (TOK, CHIPS), 1)).astype(F32)

    def keep_of(block):
        hit = jnp.max((act == block).astype(F32), axis=0, keepdims=True)
        return jnp.broadcast_to(jnp.sum(expand * hit, axis=1, keepdims=True), (TOK, FW))

    live[:, 0:FW] = keep_of(f)
    live[:, FW:PAIR] = keep_of(chip * 2 + 1 - core)

    ag_x = gather_second(ag_x1, xg, a_ssem, a_rsem)
    small[1].wait()
    small[2].wait()
    loc[0].wait()
    swap[0].wait_recv()
    swap[1].wait_recv()
    for cp in ag_x:
        cp.wait_recv()

    pre = jnp.dot(xg[0].reshape(TOK, D), we_s[...], preferred_element_type=F32)
    bias = jnp.concatenate([be_s[0], be_s[1]], axis=1)
    pre = pre + bias
    mask = live[...] * (pre > 0).astype(F32)
    live[...] = mask
    vis[s] = (mask * pre).astype(BF16)

    def zcopy(way, hop, half):
        held = 2 if hop == 4 else hop - 1
        block = lax.rem(s - held + NZ, NZ) if way == 0 else lax.rem(s + held, NZ)
        ref = vis.at[block, pl.ds(half * HALF, HALF)]
        dev = ((up, up2), (down, down2))[way][hop == 4]
        return remote(ref, ref, b_ssem.at[way, hop - 1, half], b_rsem.at[way, hop - 1, half], dev)

    zsends = {}
    for half in (0, 1):
        for way in (0, 1):
            cp = zcopy(way, 1, half)
            cp.start()
            zsends[way, 1, half] = cp

    swap_x = remote(xg.at[0], xg.at[1], p_ssem.at[0], p_rsem.at[0], peer)
    swap_x.start()

    for l in range(NZ):
        loc[1 + l].wait()
        swap[2 + l].wait_recv()

    def add_block(block, first=False):
        @pl.loop(0, D // TILE)
        def _(j):
            col = pl.ds(pl.multiple_of(j * TILE, TILE), TILE)
            part = jnp.dot(vis[block], wd_s[block, :, col], preferred_element_type=F32)
            if first:
                acc[:, col] = part
            else:
                acc[:, col] += part

    add_block(s, True)
    for hop in (1, 2, 3):
        for half in (0, 1):
            for way in (0, 1):
                zsends[way, hop, half].wait_recv()
                for later in ((2,), (3, 4) if half == way else (3,), ())[hop - 1]:
                    cp = zcopy(way, later, half)
                    cp.start()
                    zsends[way, later, half] = cp

        @pl.when(s >= hop)
        def _():
            add_block(lax.rem(s - hop + NZ, NZ))

        @pl.when(s + hop >= NZ)
        def _():
            add_block(lax.rem(s + hop, NZ))

    for way in (0, 1):
        zsends[way, 4, way].wait_recv()

    rs1 = {}
    for axis in (0, 1):
        cols = slice(axis * HD, (axis + 1) * HD)

        @pl.when(s >= 4)
        def _():
            block = lax.rem(s + 4, NZ)
            acc[:, cols] += jnp.dot(vis[block], wd_s[block, :, cols], preferred_element_type=F32)

        rb[:, :, :, cols] = acc[:, cols].astype(BF16).reshape(NX, NY, ROWS, HD)
        for o in (2, 1, 3):
            src = rb.at[o, :, :, LEFT] if axis == 0 else rb.at[:, o, :, RIGHT]
            cp = remote(src, r1.at[axis, o - 1], c_ssem.at[0, axis, o - 1], c_rsem.at[0, axis, o - 1], along(axis, o))
            cp.start()
            rs1[axis, o] = cp
    swap_c = remote(vis.at[:, :, pl.ds(FW, FW)], cs.at[:, 1], p_ssem.at[1], p_rsem.at[1], peer)
    swap_c.start()
    cs[:, 0] = vis[:, :, 0:FW]
    xt[:, 0:TOK] = xg[0].reshape(TOK, D).T
    rs2 = {}
    for axis in (0, 1):
        for o in (1, 3, 2):
            rs1[axis, o].wait_recv()
        for o in (2, 1, 3, 0):
            at = o if axis == 0 else o * NY
            part = acc[at * ROWS:(at + 1) * ROWS, axis * HD:(axis + 1) * HD]
            for k in range(3):
                part = part + r1[axis, k, o].astype(F32)
            if o == 0:
                tot[:, axis * HD:(axis + 1) * HD] = part
            else:
                r2s[axis, o - 1] = part.astype(BF16)
                cp = remote(
                    r2s.at[axis, o - 1], r2.at[axis, o - 1], c_ssem.at[1, axis, o - 1], c_rsem.at[1, axis, o - 1], along(1 - axis, o)
                )
                cp.start()
                rs2[axis, o] = cp
    small[3].wait()
    small[4].wait()
    tot[...] += bd_s[...].astype(F32) - tg_s[...].astype(F32)
    for axis in (0, 1):
        part = tot[:, axis * HD:(axis + 1) * HD]
        for o in (1, 3, 2):
            rs2[axis, o].wait_recv()
            part = part + r2[axis, o - 1].astype(F32)
        rg[0, 0, 0, :, axis * HD:(axis + 1) * HD] = part.astype(BF16)

    ag_r1 = gather_first(rg.at[0, 0, 0], rg, e_ssem, e_rsem)
    ag_r = gather_second(ag_r1, rg, e_ssem, e_rsem)
    swap_x.wait_recv()
    xt[:, TOK:2 * TOK] = xg[1].reshape(TOK, D).T
    swap_c.wait_recv()
    for l in range(NZ):
        seen = cs[l].reshape(2 * TOK, FW).T
        ct[l] = jnp.where(s >= l, seen, jnp.zeros_like(seen))
    for cp in ag_r:
        cp.wait_recv()
    swap_r = remote(rg.at[0], rg.at[1], p_ssem.at[2], p_rsem.at[2], peer)
    swap_r.start()

    def code_grad(block):
        return lax.dot_general(
            rg[0].reshape(TOK, D), wd_s[block], (((1,), (1,)), ((), ())), preferred_element_type=F32
        )

    def gcopy(way, j, half):
        return remote(
            zsb.at[way, j - 1, half], zrb.at[way, j - 1, half],
            g_ssem.at[way, j - 1, half], g_rsem.at[way, j - 1, half], ((down, down2), (up, up2))[way][j == 4],
        )

    gsends = {}
    for j in (4, 3, 2, 1):
        for way in (0, 1):
            if way == 0:
                block, given = lax.rem(s - j + NZ, NZ), s >= j
            else:
                block, given = lax.rem(s + j, NZ), s + j >= NZ
            if j == 4:
                if way == 0:
                    acc[:, 0:PAIR] = jnp.where(given, code_grad(block), 0.0)
                part = acc[way * HALF:(way + 1) * HALF, 0:PAIR]
                parts = {way: part}
            else:
                acc[:, 0:PAIR] = jnp.where(given, code_grad(block), 0.0)
                parts = {h: acc[h * HALF:(h + 1) * HALF, 0:PAIR] for h in (way, 1 - way)}
            for half, part in parts.items():
                for k in {2: (4, 3) if half == way else (3,), 1: (2,)}.get(j, ()):
                    gsends[way, k, half].wait_recv()
                    part = part + zrb[way, k - 1, half].astype(F32)
                zsb[way, j - 1, half] = part.astype(BF16)
                cp = gcopy(way, j, half)
                cp.start()
                gsends[way, j, half] = cp

    acc[:, 0:PAIR] = code_grad(s)
    swap_r.wait_recv()
    outs = []
    for j in range(D // TILE):
        col = slice(j * TILE, (j + 1) * TILE)
        part = jnp.dot(
            ct[...].reshape(NZ * FW, 2 * TOK), rg[...].reshape(2 * TOK, D)[:, col], preferred_element_type=F32
        )
        dg_ref[:, :, col] = part.astype(BF16).reshape(NZ, FW, TILE)
    for half in (0, 1):
        rows = slice(half * HALF, (half + 1) * HALF)
        own = acc[rows, 0:PAIR]
        for way in (0, 1):
            gsends[way, 1, half].wait_recv()
            own = own + zrb[way, 0, half].astype(F32)
        grad = (own * live[rows, :]).astype(BF16)
        pg_s[0, 0, rows, :] = grad[:, 0:FW]
        pg_s[1, 0, rows, :] = grad[:, FW:PAIR]
    swap_g = remote(pg_s.at[1, 0], pg_s.at[0, 1], p_ssem.at[3], p_rsem.at[3], peer)
    swap_g.start()
    swap_g.wait_recv()
    pg = pg_s[0].reshape(2 * TOK, FW)
    eg_ref[...] = jnp.dot(xt[...], pg, preferred_element_type=F32).astype(BF16)
    bg_ref[...] = jnp.sum(pg.astype(F32), axis=0, keepdims=True)

    for cp in list(ag_x1.values()) + list(ag_r1.values()) + list(rs1.values()) + list(rs2.values()):
        cp.wait_send()
    for cp in ag_x + ag_r + swap + [swap_x, swap_c, swap_r, swap_g]:
        cp.wait_send()
    for cp in list(zsends.values()) + list(gsends.values()):
        cp.wait_send()
    for cp in outs:
        cp.wait()


def fused(x, we, be, wd, bd, tg, act):
    vmem = pl.BlockSpec(memory_space=pltpu.VMEM)
    hbm = pl.BlockSpec(memory_space=pl.ANY)
    dma = pltpu.SemaphoreType.DMA
    return pl.pallas_call(
        step_kernel,
        name="step",
        out_shape=(
            pltpu.VMEM((D, FW), BF16),
            pltpu.VMEM((1, FW), F32),
            pltpu.VMEM((NZ, FW, D), BF16),
        ),
        in_specs=[pl.BlockSpec(memory_space=pltpu.HBM)] * 7,
        out_specs=(vmem, vmem, vmem),
        scratch_shapes=[
            pltpu.VMEM((2, NX, NY, ROWS, D), BF16),
            pltpu.VMEM((2, NX, NY, ROWS, D), BF16),
            pltpu.VMEM((D, PAIR), BF16),
            pltpu.VMEM((NZ, PAIR, D), BF16),
            pltpu.VMEM((2, 1, FW), F32),
            pltpu.VMEM((1, D), BF16),
            pltpu.VMEM((ROWS, D), BF16),
            pltpu.VMEM((8, CHIPS), jnp.int32),
            pltpu.VMEM((NZ, TOK, PAIR), BF16),
            pltpu.VMEM((TOK, PAIR), F32),
            pltpu.VMEM((TOK, D), F32),
            pltpu.VMEM((NX, NY, ROWS, D), BF16),
            pltpu.VMEM((2, 3, 4, ROWS, HD), BF16),
            pltpu.VMEM((2, 3, ROWS, HD), BF16),
            pltpu.VMEM((2, 3, ROWS, HD), BF16),
            pltpu.VMEM((ROWS, D), F32),
            pltpu.VMEM((NZ, 2, TOK, FW), BF16),
            pltpu.VMEM((NZ, FW, 2 * TOK), BF16),
            pltpu.VMEM((D, 2 * TOK), BF16),
            pltpu.VMEM((2, 2, TOK, FW), BF16),
            pltpu.VMEM((2, 4, 2, HALF, PAIR), BF16),
            pltpu.VMEM((2, 4, 2, HALF, PAIR), BF16),
            dma((NZ + 1,)), dma((NZ + 2,)), dma((NZ + 2,)),
            dma((2, 2, 3)), dma((2, 2, 3)),
            dma((2, 4, 2)), dma((2, 4, 2)),
            dma((2, 2, 3)), dma((2, 2, 3)),
            dma((2, 2, 3)), dma((2, 2, 3)),
            dma((2, 4, 2)), dma((2, 4, 2)),
            dma((4,)), dma((4,)),
            dma((5,)),
        ],
        compiler_params=pltpu.CompilerParams(
            collective_id=0, has_side_effects=True, vmem_limit_bytes=44 * 2**20
        ),
    )(x, we, be, wd, bd, tg, act)


def store_kernel(e_ref, b_ref, d_ref, eo_ref, bo_ref, do_ref, sem):
    copies = [pltpu.make_async_copy(e_ref, eo_ref, sem.at[0]), pltpu.make_async_copy(b_ref, bo_ref, sem.at[1])]
    copies += [pltpu.make_async_copy(d_ref.at[l], do_ref.at[l], sem.at[2 + l]) for l in range(NZ)]
    for cp in copies:
        cp.start()
    for cp in copies:
        cp.wait()


def store(e, b, d):
    hbm = pl.BlockSpec(memory_space=pl.ANY)
    return pl.pallas_call(
        store_kernel,
        name="store",
        out_shape=tuple(jax.ShapeDtypeStruct(a.shape, a.dtype) for a in (e, b, d)),
        in_specs=[hbm] * 3,
        out_specs=(hbm,) * 3,
        scratch_shapes=[pltpu.SemaphoreType.DMA((2 + NZ,))],
        compiler_params=pltpu.CompilerParams(vmem_limit_bytes=2**20),
    )(e, b, d)


def body(inputs, enc_weight, enc_bias, dec_weight, dec_bias, target, active):
    args = (inputs[0], enc_weight[0], enc_bias, dec_weight[0], dec_bias, target[0], active[0].T)
    enc_grad, bias_grad, dec_grad = fused(*(pltpu.with_memory_space_constraint(a, pltpu.HBM) for a in args))
    enc_grad, bias_grad, dec_grad = store(enc_grad, bias_grad, dec_grad)
    return enc_grad[None], bias_grad, dec_grad[None]


def solution(mesh):
    return jax.shard_map(
        body,
        mesh=mesh,
        in_specs=(
            P("section", "feat", None),
            P("section", None, "feat"),
            P("section", "feat"),
            P("section", None, "feat", None),
            P("section", None),
            P("section", "feat", None),
            P("section", None, None),
        ),
        out_specs=(
            P("section", None, "feat"),
            P("section", "feat"),
            P("section", None, "feat", None),
        ),
        check_vma=False,
    )
```

```python
import functools

import jax
import jax.numpy as jnp
from jax import lax
from jax.experimental import pallas as pl
from jax.experimental.pallas import tpu as pltpu
from jax.sharding import PartitionSpec as P

MESH = pl.DeviceIdType.MESH
BF16 = jnp.bfloat16
F32 = jnp.float32

NX = 4
NY = 4
CHIPS = NX * NY
NZ = 8
ROWS = 16
FW = 128
D = 2560
TOK = CHIPS * ROWS
PAIR = 2 * FW
CUTS = 4
PIECE = TOK // CUTS
TILE = 512

HD = D // 2
QW = HD // 2
PARTS = [(axis, q) for q in (0, 1) for axis in (0, 1)]


def step_kernel(
    x_ref, we_ref, be_ref, wd_ref, bd_ref, tg_ref, act_ref,
    eg_ref, bg_ref, dg_ref,
    xg, rg, we_s, wd_s, be_s, bd_s, tg_s, act_s, vis, live, acc, rb, r1, r2s, r2, lhs, tot, cs, ct, xt, pg_s, zsb, zrb,
    in_sem, in_ssem, in_rsem, a_ssem, a_rsem, b_ssem, b_rsem, c_ssem, c_rsem,
    e_ssem, e_rsem, g_ssem, g_rsem, p_ssem, p_rsem, small_sem,
):
    s = lax.axis_index("section")
    f = lax.axis_index("feat")
    core = lax.rem(f, 2)
    chip = lax.div(f, 2)
    cx = lax.div(chip, NY)
    cy = lax.rem(chip, NY)

    def along(axis, step):
        x = lax.rem(cx + step, NX) if axis == 0 else cx
        y = lax.rem(cy + step, NY) if axis == 1 else cy
        return {"section": s, "feat": (x * NY + y) * 2 + core}

    peer = {"section": s, "feat": chip * 2 + 1 - core}
    up = {"section": lax.rem(s + 1, NZ), "feat": f}
    down = {"section": lax.rem(s + NZ - 1, NZ), "feat": f}
    up2 = {"section": lax.rem(s + 2, NZ), "feat": f}
    down2 = {"section": lax.rem(s + NZ - 2, NZ), "feat": f}

    def remote(src, dst, ssem, rsem, dev):
        return pltpu.make_async_remote_copy(
            src_ref=src, dst_ref=dst, send_sem=ssem, recv_sem=rsem, device_id=dev, device_id_type=MESH
        )

    barrier = pltpu.get_barrier_semaphore()
    for dev in [peer, up, down, up2, down2] + [along(axis, o) for axis in (0, 1) for o in (1, 2, 3)]:
        pl.semaphore_signal(barrier, inc=1, device_id=dev, device_id_type=MESH)

    loc = [pltpu.make_async_copy(we_ref, we_s.at[:, pl.ds(0, FW)], in_sem.at[NZ])]
    for l in range(NZ):
        loc.append(pltpu.make_async_copy(wd_ref.at[l], wd_s.at[l, pl.ds(0, FW)], in_sem.at[l]))
    small = [
        pltpu.make_async_copy(a, b, small_sem.at[k])
        for k, (a, b) in enumerate(
            [(act_ref, act_s), (be_ref, be_s.at[0]), (x_ref, xg.at[0, 0, 0]), (bd_ref, bd_s), (tg_ref, tg_s)]
        )
    ]
    for cp in small + loc:
        cp.start()

    pl.semaphore_wait(barrier, 11)

    def columns(axis, q):
        return pl.ds(axis * HD + q * QW, QW)

    def gather_first(axis, q, src, g, ssem, rsem):
        copies = {}
        for turn, way in ((0, axis), (1, 1 - axis)):
            for o in (2, 1, 3):
                there = (NX - o, 0) if way == 0 else (0, NY - o)
                cols = columns(axis, q)
                cp = remote(
                    src.at[:, cols], g.at[0, there[0], there[1], :, cols],
                    ssem.at[turn, q, axis, o - 1], rsem.at[turn, q, axis, o - 1], along(way, o),
                )
                cp.start()
                copies[turn, o] = cp
        return copies

    def gather_second(axis, q, first, g, ssem, rsem):
        copies = []
        for o in (1, 3, 2):
            first[0, o].wait_recv()
        for o in (2, 1, 3):
            cols = columns(axis, q)
            if axis == 0:
                src, dst = g.at[0, pl.ds(1, 3), 0, :, cols], g.at[0, pl.ds(1, 3), NY - o, :, cols]
            else:
                src, dst = g.at[0, 0, pl.ds(1, 3), :, cols], g.at[0, NX - o, pl.ds(1, 3), :, cols]
            cp = remote(src, dst, ssem.at[2, q, axis, o - 1], rsem.at[2, q, axis, o - 1], along(1 - axis, o))
            cp.start()
            copies.append(cp)
        return copies

    def gather_end(q, first, second):
        for axis in (0, 1):
            for o in (1, 3, 2):
                first[axis, q][1, o].wait_recv()
            for cp in second[axis, q]:
                cp.wait_recv()

    ag_x1 = {p: gather_first(*p, x_ref, xg, a_ssem, a_rsem) for p in PARTS}
    swap = [
        remote(we_ref, we_s.at[:, pl.ds(FW, FW)], in_ssem.at[NZ], in_rsem.at[NZ], peer),
        remote(be_ref, be_s.at[1], in_ssem.at[NZ + 1], in_rsem.at[NZ + 1], peer),
    ]
    for l in range(NZ):
        swap.append(remote(wd_ref.at[l], wd_s.at[l, pl.ds(FW, FW)], in_ssem.at[l], in_rsem.at[l], peer))
    for cp in swap:
        cp.start()

    small[0].wait()
    act = act_s[...]
    row_at = lax.broadcasted_iota(jnp.int32, (TOK, CHIPS), 0) // ROWS
    row_chip = lax.rem(cx + row_at // NY, NX) * NY + lax.rem(cy + lax.rem(row_at, NY), NY)
    expand = (row_chip == lax.broadcasted_iota(jnp.int32, (TOK, CHIPS), 1)).astype(F32)

    def keep_of(block):
        hit = jnp.max((act == block).astype(F32), axis=0, keepdims=True)
        return jnp.broadcast_to(jnp.sum(expand * hit, axis=1, keepdims=True), (TOK, FW))

    live[:, 0:FW] = keep_of(f)
    live[:, FW:PAIR] = keep_of(chip * 2 + 1 - core)

    ag_x = {p: gather_second(*p, ag_x1[p], xg, a_ssem, a_rsem) for p in PARTS}
    small[1].wait()
    small[2].wait()
    loc[0].wait()
    swap[0].wait_recv()
    swap[1].wait_recv()
    def pre_part(q, first, last):
        total = None
        for axis in (0, 1):
            at = axis * HD + q * QW
            x = xg[0, first:last, :, :, at:at + QW].reshape((last - first) * NY * ROWS, QW)
            part = jnp.dot(x, we_s[at:at + QW, :], preferred_element_type=F32)
            total = part if total is None else total + part
        return total

    def zcopy(way, hop, piece):
        held = 2 if hop == 4 else hop - 1
        block = lax.rem(s - held + NZ, NZ) if way == 0 else lax.rem(s + held, NZ)
        ref = vis.at[block, pl.ds(piece * PIECE, PIECE)]
        dev = ((up, up2), (down, down2))[way][hop == 4]
        return remote(ref, ref, b_ssem.at[way, hop - 1, piece], b_rsem.at[way, hop - 1, piece], dev)

    zsends = {}
    gather_end(0, ag_x1, ag_x)
    acc[:, 0:PAIR] = pre_part(0, 0, NX)
    bias = jnp.concatenate([be_s[0], be_s[1]], axis=1)
    gather_end(1, ag_x1, ag_x)
    for half in (0, 1):
        rows = slice(half * TOK // 2, (half + 1) * TOK // 2)
        pre = acc[rows, 0:PAIR] + pre_part(1, half * NX // 2, (half + 1) * NX // 2) + bias
        mask = live[rows, :] * (pre > 0).astype(F32)
        live[rows, :] = mask
        vis[s, rows, :] = (mask * pre).astype(BF16)
        for piece in range(half * CUTS // 2, (half + 1) * CUTS // 2):
            for way in (0, 1):
                cp = zcopy(way, 1, piece)
                cp.start()
                zsends[way, 1, piece] = cp

    swap_x = remote(xg.at[0], xg.at[1], p_ssem.at[0], p_rsem.at[0], peer)
    swap_x.start()

    for l in range(NZ):
        loc[1 + l].wait()
        swap[2 + l].wait_recv()

    def add_block(block, first=False):
        @pl.loop(0, D // TILE)
        def _(j):
            col = pl.ds(pl.multiple_of(j * TILE, TILE), TILE)
            part = jnp.dot(vis[block], wd_s[block, :, col], preferred_element_type=F32)
            if first:
                acc[:, col] = part
            else:
                acc[:, col] += part

    add_block(s, True)
    for hop in (1, 2, 3):
        for piece in range(CUTS):
            for way in (0, 1):
                zsends[way, hop, piece].wait_recv()
                for later in ((2,), (3, 4) if piece * 2 // CUTS == way else (3,), ())[hop - 1]:
                    cp = zcopy(way, later, piece)
                    cp.start()
                    zsends[way, later, piece] = cp

        if hop < 3:

            @pl.when(s >= hop)
            def _():
                add_block(lax.rem(s - hop + NZ, NZ))

            @pl.when(s + hop >= NZ)
            def _():
                add_block(lax.rem(s + hop, NZ))

    for way in (0, 1):
        for piece in range(way * CUTS // 2, (way + 1) * CUTS // 2):
            zsends[way, 4, piece].wait_recv()
    last = [(lax.rem(s + NZ - 3, NZ), s >= 3), (lax.rem(s + 3, NZ), s + 3 >= NZ), (lax.rem(s + 4, NZ), s >= 4)]
    for k, (block, given) in enumerate(last):
        codes = vis[block]
        lhs[:, k * PAIR:(k + 1) * PAIR] = jnp.where(given, codes, jnp.zeros_like(codes))

    rs1 = {}
    for axis, q in PARTS:
        at = axis * HD + q * QW
        cols = slice(at, at + QW)
        rhs = jnp.concatenate([wd_s[block, :, cols] for block, _ in last], axis=0)
        part = acc[:, cols] + jnp.dot(lhs[...], rhs, preferred_element_type=F32)
        acc[:, cols] = part
        rb[:, :, :, cols] = part.astype(BF16).reshape(NX, NY, ROWS, QW)
        for o in (2, 1, 3):
            src = rb.at[o, :, :, columns(axis, q)] if axis == 0 else rb.at[:, o, :, columns(axis, q)]
            cp = remote(
                src, r1.at[axis, q, o - 1], c_ssem.at[0, q, axis, o - 1], c_rsem.at[0, q, axis, o - 1], along(axis, o)
            )
            cp.start()
            rs1[axis, q, o] = cp
    swap_c = remote(vis.at[:, :, pl.ds(FW, FW)], cs.at[:, 1], p_ssem.at[1], p_rsem.at[1], peer)
    swap_c.start()
    cs[:, 0] = vis[:, :, 0:FW]
    xt[:, 0:TOK] = xg[0].reshape(TOK, D).T
    small[3].wait()
    small[4].wait()
    rs2 = {}
    for axis, q in PARTS:
        at = axis * HD + q * QW
        cols = slice(at, at + QW)
        for o in (1, 3, 2):
            rs1[axis, q, o].wait_recv()
        for o in (2, 1, 3, 0):
            row = (o if axis == 0 else o * NY) * ROWS
            part = acc[row:row + ROWS, cols]
            for k in range(3):
                part = part + r1[axis, q, k, o].astype(F32)
            if o == 0:
                tot[:, cols] = part + bd_s[:, cols].astype(F32) - tg_s[:, cols].astype(F32)
            else:
                r2s[axis, q, o - 1] = part.astype(BF16)
                cp = remote(
                    r2s.at[axis, q, o - 1], r2.at[axis, q, o - 1],
                    c_ssem.at[1, q, axis, o - 1], c_rsem.at[1, q, axis, o - 1], along(1 - axis, o),
                )
                cp.start()
                rs2[axis, q, o] = cp

    ag_r1 = {}
    for axis, q in PARTS:
        at = axis * HD + q * QW
        cols = slice(at, at + QW)
        part = tot[:, cols]
        for o in (1, 3, 2):
            rs2[axis, q, o].wait_recv()
            part = part + r2[axis, q, o - 1].astype(F32)
        rg[0, 0, 0, :, cols] = part.astype(BF16)
        ag_r1[axis, q] = gather_first(axis, q, rg.at[0, 0, 0], rg, e_ssem, e_rsem)
    ag_r = {p: gather_second(*p, ag_r1[p], rg, e_ssem, e_rsem) for p in PARTS}
    swap_x.wait_recv()
    xt[:, TOK:2 * TOK] = xg[1].reshape(TOK, D).T
    swap_c.wait_recv()
    for l in range(NZ):
        seen = cs[l].reshape(2 * TOK, FW).T
        ct[l] = jnp.where(s >= l, seen, jnp.zeros_like(seen))
    def grad_cols(block, at, width):
        return lax.dot_general(
            rg[0, :, :, :, at:at + width].reshape(TOK, width), wd_s[block, :, at:at + width],
            (((1,), (1,)), ((), ())), preferred_element_type=F32,
        )

    def grad_part(block, q):
        return grad_cols(block, q * QW, QW) + grad_cols(block, HD + q * QW, QW)

    def far(way, j):
        if way == 0:
            return lax.rem(s - j + NZ, NZ), s >= j
        return lax.rem(s + j, NZ), s + j >= NZ

    def gcopy(way, j, piece):
        return remote(
            zsb.at[way, j - 1, piece], zrb.at[way, j - 1, piece],
            g_ssem.at[way, j - 1, piece], g_rsem.at[way, j - 1, piece], ((down, down2), (up, up2))[way][j == 4],
        )

    gsends = {}

    def pass_on(way, j, piece, slot, given):
        part = jnp.where(given, acc[piece * PIECE:(piece + 1) * PIECE, slot * PAIR:(slot + 1) * PAIR], 0.0)
        for k in {2: (4, 3) if piece * 2 // CUTS == way else (3,), 1: (2,)}.get(j, ()):
            gsends[way, k, piece].wait_recv()
            part = part + zrb[way, k - 1, piece].astype(F32)
        zsb[way, j - 1, piece] = part.astype(BF16)
        cp = gcopy(way, j, piece)
        cp.start()
        gsends[way, j, piece] = cp

    gather_end(0, ag_r1, ag_r)
    for way in (0, 1):
        acc[:, way * PAIR:(way + 1) * PAIR] = grad_part(far(way, 3)[0], 0)
    gather_end(1, ag_r1, ag_r)
    for way in (0, 1):
        acc[:, way * PAIR:(way + 1) * PAIR] += grad_part(far(way, 3)[0], 1)
        for piece in range(CUTS):
            pass_on(way, 3, piece, way, far(way, 3)[1])
    acc[:, 0:PAIR] = grad_cols(far(0, 4)[0], 0, D)
    for piece in range(CUTS):
        pass_on(piece * 2 // CUTS, 4, piece, 0, far(0, 4)[1])
    swap_r = remote(rg.at[0], rg.at[1], p_ssem.at[2], p_rsem.at[2], peer)
    swap_r.start()

    def dec_tile(j):
        col = slice(j * TILE, (j + 1) * TILE)
        part = jnp.dot(
            ct[...].reshape(NZ * FW, 2 * TOK), rg[...].reshape(2 * TOK, D)[:, col], preferred_element_type=F32
        )
        dg_ref[:, :, col] = part.astype(BF16).reshape(NZ, FW, TILE)

    for j in (2, 1):
        for way in (0, 1):
            acc[:, way * PAIR:(way + 1) * PAIR] = grad_cols(far(way, j)[0], 0, D)
        if j == 1:
            swap_r.wait_recv()
            dec_tile(0)
        for piece in range(CUTS):
            for way in (0, 1):
                pass_on(way, j, piece, way, far(way, j)[1])

    acc[:, 0:PAIR] = grad_cols(s, 0, D)
    for j in range(1, D // TILE):
        dec_tile(j)
    for piece in range(CUTS):
        rows = slice(piece * PIECE, (piece + 1) * PIECE)
        own = acc[rows, 0:PAIR]
        for way in (0, 1):
            gsends[way, 1, piece].wait_recv()
            own = own + zrb[way, 0, piece].astype(F32)
        grad = (own * live[rows, :]).astype(BF16)
        pg_s[0, 0, rows, :] = grad[:, 0:FW]
        pg_s[1, 0, rows, :] = grad[:, FW:PAIR]
    swap_g = remote(pg_s.at[1, 0], pg_s.at[0, 1], p_ssem.at[3], p_rsem.at[3], peer)
    swap_g.start()
    own = jnp.dot(xt[:, 0:TOK], pg_s[0, 0], preferred_element_type=F32)
    swap_g.wait_recv()
    eg_ref[...] = (own + jnp.dot(xt[:, TOK:2 * TOK], pg_s[0, 1], preferred_element_type=F32)).astype(BF16)
    bg_ref[...] = jnp.sum(pg_s[0].reshape(2 * TOK, FW).astype(F32), axis=0, keepdims=True)

    for first in list(ag_x1.values()) + list(ag_r1.values()):
        for cp in first.values():
            cp.wait_send()
    for cp in list(rs1.values()) + list(rs2.values()):
        cp.wait_send()
    for copies in list(ag_x.values()) + list(ag_r.values()):
        for cp in copies:
            cp.wait_send()
    for cp in swap + [swap_x, swap_c, swap_r, swap_g]:
        cp.wait_send()
    for cp in list(zsends.values()) + list(gsends.values()):
        cp.wait_send()


def fused(x, we, be, wd, bd, tg, act):
    vmem = pl.BlockSpec(memory_space=pltpu.VMEM)
    hbm = pl.BlockSpec(memory_space=pl.ANY)
    dma = pltpu.SemaphoreType.DMA
    return pl.pallas_call(
        step_kernel,
        name="step",
        out_shape=(
            pltpu.VMEM((D, FW), BF16),
            pltpu.VMEM((1, FW), F32),
            pltpu.VMEM((NZ, FW, D), BF16),
        ),
        in_specs=[pl.BlockSpec(memory_space=pltpu.HBM)] * 7,
        out_specs=(vmem, vmem, vmem),
        scratch_shapes=[
            pltpu.VMEM((2, NX, NY, ROWS, D), BF16),
            pltpu.VMEM((2, NX, NY, ROWS, D), BF16),
            pltpu.VMEM((D, PAIR), BF16),
            pltpu.VMEM((NZ, PAIR, D), BF16),
            pltpu.VMEM((2, 1, FW), F32),
            pltpu.VMEM((1, D), BF16),
            pltpu.VMEM((ROWS, D), BF16),
            pltpu.VMEM((8, CHIPS), jnp.int32),
            pltpu.VMEM((NZ, TOK, PAIR), BF16),
            pltpu.VMEM((TOK, PAIR), F32),
            pltpu.VMEM((TOK, D), F32),
            pltpu.VMEM((NX, NY, ROWS, D), BF16),
            pltpu.VMEM((2, 2, 3, 4, ROWS, QW), BF16),
            pltpu.VMEM((2, 2, 3, ROWS, QW), BF16),
            pltpu.VMEM((2, 2, 3, ROWS, QW), BF16),
            pltpu.VMEM((TOK, 3 * PAIR), BF16),
            pltpu.VMEM((ROWS, D), F32),
            pltpu.VMEM((NZ, 2, TOK, FW), BF16),
            pltpu.VMEM((NZ, FW, 2 * TOK), BF16),
            pltpu.VMEM((D, 2 * TOK), BF16),
            pltpu.VMEM((2, 2, TOK, FW), BF16),
            pltpu.VMEM((2, 4, CUTS, PIECE, PAIR), BF16),
            pltpu.VMEM((2, 4, CUTS, PIECE, PAIR), BF16),
            dma((NZ + 1,)), dma((NZ + 2,)), dma((NZ + 2,)),
            dma((3, 2, 2, 3)), dma((3, 2, 2, 3)),
            dma((2, 4, CUTS)), dma((2, 4, CUTS)),
            dma((3, 2, 2, 3)), dma((3, 2, 2, 3)),
            dma((3, 2, 2, 3)), dma((3, 2, 2, 3)),
            dma((2, 4, CUTS)), dma((2, 4, CUTS)),
            dma((4,)), dma((4,)),
            dma((5,)),
        ],
        compiler_params=pltpu.CompilerParams(
            collective_id=0, has_side_effects=True, vmem_limit_bytes=44 * 2**20
        ),
    )(x, we, be, wd, bd, tg, act)


def store_kernel(e_ref, b_ref, d_ref, eo_ref, bo_ref, do_ref, sem):
    copies = [pltpu.make_async_copy(e_ref, eo_ref, sem.at[0]), pltpu.make_async_copy(b_ref, bo_ref, sem.at[1])]
    copies += [pltpu.make_async_copy(d_ref.at[l], do_ref.at[l], sem.at[2 + l]) for l in range(NZ)]
    for cp in copies:
        cp.start()
    for cp in copies:
        cp.wait()


def store(e, b, d):
    hbm = pl.BlockSpec(memory_space=pl.ANY)
    return pl.pallas_call(
        store_kernel,
        name="store",
        out_shape=tuple(jax.ShapeDtypeStruct(a.shape, a.dtype) for a in (e, b, d)),
        in_specs=[hbm] * 3,
        out_specs=(hbm,) * 3,
        scratch_shapes=[pltpu.SemaphoreType.DMA((2 + NZ,))],
        compiler_params=pltpu.CompilerParams(vmem_limit_bytes=2**20),
    )(e, b, d)


def body(inputs, enc_weight, enc_bias, dec_weight, dec_bias, target, active):
    args = (inputs[0], enc_weight[0], enc_bias, dec_weight[0], dec_bias, target[0], active[0].T)
    enc_grad, bias_grad, dec_grad = fused(*(pltpu.with_memory_space_constraint(a, pltpu.HBM) for a in args))
    enc_grad, bias_grad, dec_grad = store(enc_grad, bias_grad, dec_grad)
    return enc_grad[None], bias_grad, dec_grad[None]


def solution(mesh):
    return jax.shard_map(
        body,
        mesh=mesh,
        in_specs=(
            P("section", "feat", None),
            P("section", None, "feat"),
            P("section", "feat"),
            P("section", None, "feat", None),
            P("section", None),
            P("section", "feat", None),
            P("section", None, None),
        ),
        out_specs=(
            P("section", None, "feat"),
            P("section", "feat"),
            P("section", None, "feat", None),
        ),
        check_vma=False,
    )
```

```python
import functools

import jax
import jax.numpy as jnp
from jax import lax
from jax.experimental import pallas as pl
from jax.experimental.pallas import tpu as pltpu
from jax.sharding import PartitionSpec as P

MESH = pl.DeviceIdType.MESH
BF16 = jnp.bfloat16
F32 = jnp.float32

NX = 4
NY = 4
CHIPS = NX * NY
NZ = 8
ROWS = 16
FW = 128
D = 2560
TOK = CHIPS * ROWS
PAIR = 2 * FW
CUTS = 4
PIECE = TOK // CUTS
TILE = 512

HD = D // 2
QW = HD // 2
PARTS = [(axis, q) for q in (0, 1) for axis in (0, 1)]


def step_kernel(
    x_ref, we_ref, be_ref, wd_ref, bd_ref, tg_ref, act_ref,
    eg_ref, bg_ref, dg_ref,
    xg, rg, we_s, wd_s, be_s, bd_s, tg_s, act_s, vis, live, acc, rb, r1, r2s, r2, lhs, tot, cs, ct, xt, pg_s, zsb, zrb,
    in_sem, in_ssem, in_rsem, a_ssem, a_rsem, a2_ssem, a2_rsem, b_ssem, b_rsem, c_ssem, c_rsem,
    e_ssem, e_rsem, g_ssem, g_rsem, p_ssem, p_rsem, small_sem,
):
    s = lax.axis_index("section")
    f = lax.axis_index("feat")
    core = lax.rem(f, 2)
    chip = lax.div(f, 2)
    cx = lax.div(chip, NY)
    cy = lax.rem(chip, NY)

    def along(axis, step):
        x = lax.rem(cx + step, NX) if axis == 0 else cx
        y = lax.rem(cy + step, NY) if axis == 1 else cy
        return {"section": s, "feat": (x * NY + y) * 2 + core}

    peer = {"section": s, "feat": chip * 2 + 1 - core}
    up = {"section": lax.rem(s + 1, NZ), "feat": f}
    down = {"section": lax.rem(s + NZ - 1, NZ), "feat": f}
    up2 = {"section": lax.rem(s + 2, NZ), "feat": f}
    down2 = {"section": lax.rem(s + NZ - 2, NZ), "feat": f}

    def remote(src, dst, ssem, rsem, dev):
        return pltpu.make_async_remote_copy(
            src_ref=src, dst_ref=dst, send_sem=ssem, recv_sem=rsem, device_id=dev, device_id_type=MESH
        )

    barrier = pltpu.get_barrier_semaphore()
    for dev in [peer, up, down, up2, down2] + [along(axis, o) for axis in (0, 1) for o in (1, 2, 3)]:
        pl.semaphore_signal(barrier, inc=1, device_id=dev, device_id_type=MESH)

    loc = [pltpu.make_async_copy(we_ref, we_s.at[:, pl.ds(0, FW)], in_sem.at[NZ])]
    for l in range(NZ):
        loc.append(pltpu.make_async_copy(wd_ref.at[l], wd_s.at[l, pl.ds(0, FW)], in_sem.at[l]))
    small = [
        pltpu.make_async_copy(a, b, small_sem.at[k])
        for k, (a, b) in enumerate(
            [(act_ref, act_s), (be_ref, be_s.at[0]), (x_ref, xg.at[0, 0, 0]), (bd_ref, bd_s), (tg_ref, tg_s)]
        )
    ]
    for cp in small + loc:
        cp.start()

    pl.semaphore_wait(barrier, 11)

    def columns(axis, q):
        return pl.ds(axis * HD + q * QW, QW)

    def gather_first(axis, q, src, g, ssem, rsem, turns=(0, 1), copies=None):
        copies = {} if copies is None else copies
        for turn in turns:
            way = axis if turn == 0 else 1 - axis
            for o in (2, 1, 3):
                there = (NX - o, 0) if way == 0 else (0, NY - o)
                cols = columns(axis, q)
                cp = remote(
                    src.at[:, cols], g.at[0, there[0], there[1], :, cols],
                    ssem.at[turn, q, axis, o - 1], rsem.at[turn, q, axis, o - 1], along(way, o),
                )
                cp.start()
                copies[turn, o] = cp
        return copies

    def gather_second(half, first, g, ssem, rsem):
        copies = {}
        for axis, q in [(a, b) for b in (0, 1) for a in (0, 1)]:
            cols = columns(axis, q)
            if axis == 0:
                for o in ((3,), (1, 2))[half]:
                    first[axis, q][0, o].wait_recv()
                at, count = ((1, 1), (2, 2))[half]
                for o in (2, 1, 3):
                    src, dst = g.at[0, pl.ds(at, count), 0, :, cols], g.at[0, pl.ds(at, count), NY - o, :, cols]
                    k = half * 3 + o - 1
                    copies[axis, q, o] = remote(src, dst, ssem.at[q, axis, k], rsem.at[q, axis, k], along(1, o))
                    copies[axis, q, o].start()
            else:
                if half == 0:
                    for o in (1, 3, 2):
                        first[axis, q][0, o].wait_recv()
                for o in ((3,), (2, 1))[half]:
                    src, dst = g.at[0, 0, pl.ds(1, 3), :, cols], g.at[0, NX - o, pl.ds(1, 3), :, cols]
                    copies[axis, q, o] = remote(src, dst, ssem.at[q, axis, o - 1], rsem.at[q, axis, o - 1], along(0, o))
                    copies[axis, q, o].start()
        return copies

    def gather_end(half, first, second):
        for q in (0, 1):
            if half == 0:
                for o in (1, 3, 2):
                    first[0, q][1, o].wait_recv()
            for o in ((3,), (1, 2))[half]:
                first[1, q][1, o].wait_recv()
        for cp in second[half].values():
            cp.wait_recv()

    def gather_second_q(axis, q, first, g, ssem, rsem):
        copies = []
        for o in (1, 3, 2):
            first[0, o].wait_recv()
        for o in (2, 1, 3):
            cols = columns(axis, q)
            if axis == 0:
                src, dst = g.at[0, pl.ds(1, 3), 0, :, cols], g.at[0, pl.ds(1, 3), NY - o, :, cols]
            else:
                src, dst = g.at[0, 0, pl.ds(1, 3), :, cols], g.at[0, NX - o, pl.ds(1, 3), :, cols]
            cp = remote(src, dst, ssem.at[2, q, axis, o - 1], rsem.at[2, q, axis, o - 1], along(1 - axis, o))
            cp.start()
            copies.append(cp)
        return copies

    def gather_end_q(q, first, second):
        for axis in (0, 1):
            for o in (1, 3, 2):
                first[axis, q][1, o].wait_recv()
            for cp in second[axis, q]:
                cp.wait_recv()

    ag_x1 = {p: gather_first(*p, x_ref, xg, a_ssem, a_rsem, (0,)) for p in PARTS}
    for p in PARTS:
        gather_first(*p, x_ref, xg, a_ssem, a_rsem, (1,), ag_x1[p])
    swap = [
        remote(we_ref, we_s.at[:, pl.ds(FW, FW)], in_ssem.at[NZ], in_rsem.at[NZ], peer),
        remote(be_ref, be_s.at[1], in_ssem.at[NZ + 1], in_rsem.at[NZ + 1], peer),
    ]
    for l in range(NZ):
        swap.append(remote(wd_ref.at[l], wd_s.at[l, pl.ds(FW, FW)], in_ssem.at[l], in_rsem.at[l], peer))
    for cp in swap:
        cp.start()

    small[0].wait()
    act = act_s[...]
    row_at = lax.broadcasted_iota(jnp.int32, (TOK, CHIPS), 0) // ROWS
    row_chip = lax.rem(cx + row_at // NY, NX) * NY + lax.rem(cy + lax.rem(row_at, NY), NY)
    expand = (row_chip == lax.broadcasted_iota(jnp.int32, (TOK, CHIPS), 1)).astype(F32)

    def keep_of(block):
        hit = jnp.max((act == block).astype(F32), axis=0, keepdims=True)
        return jnp.broadcast_to(jnp.sum(expand * hit, axis=1, keepdims=True), (TOK, FW))

    live[:, 0:FW] = keep_of(f)
    live[:, FW:PAIR] = keep_of(chip * 2 + 1 - core)

    ag_x = [gather_second(half, ag_x1, xg, a2_ssem, a2_rsem) for half in (0, 1)]
    small[1].wait()
    small[2].wait()
    loc[0].wait()
    swap[0].wait_recv()
    swap[1].wait_recv()
    def zcopy(way, hop, piece):
        held = 2 if hop == 4 else hop - 1
        block = lax.rem(s - held + NZ, NZ) if way == 0 else lax.rem(s + held, NZ)
        ref = vis.at[block, pl.ds(piece * PIECE, PIECE)]
        dev = ((up, up2), (down, down2))[way][hop == 4]
        return remote(ref, ref, b_ssem.at[way, hop - 1, piece], b_rsem.at[way, hop - 1, piece], dev)

    zsends = {}
    bias = jnp.concatenate([be_s[0], be_s[1]], axis=1)
    for half in (0, 1):
        gather_end(half, ag_x1, ag_x)
        rows = slice(half * TOK // 2, (half + 1) * TOK // 2)
        x = xg[0, half * NX // 2:(half + 1) * NX // 2].reshape(TOK // 2, D)
        pre = jnp.dot(x, we_s[...], preferred_element_type=F32) + bias
        mask = live[rows, :] * (pre > 0).astype(F32)
        live[rows, :] = mask
        vis[s, rows, :] = (mask * pre).astype(BF16)
        for piece in range(half * CUTS // 2, (half + 1) * CUTS // 2):
            for way in (0, 1):
                cp = zcopy(way, 1, piece)
                cp.start()
                zsends[way, 1, piece] = cp

    swap_x = remote(xg.at[0], xg.at[1], p_ssem.at[0], p_rsem.at[0], peer)
    swap_x.start()

    for l in range(NZ):
        loc[1 + l].wait()
        swap[2 + l].wait_recv()

    def add_block(block, first=False):
        @pl.loop(0, D // TILE)
        def _(j):
            col = pl.ds(pl.multiple_of(j * TILE, TILE), TILE)
            part = jnp.dot(vis[block], wd_s[block, :, col], preferred_element_type=F32)
            if first:
                acc[:, col] = part
            else:
                acc[:, col] += part

    add_block(s, True)
    for hop in (1, 2, 3):
        for piece in range(CUTS):
            for way in (0, 1):
                zsends[way, hop, piece].wait_recv()
                for later in ((2,), (4, 3) if piece * 2 // CUTS == way else (3,), ())[hop - 1]:
                    cp = zcopy(way, later, piece)
                    cp.start()
                    zsends[way, later, piece] = cp

        if hop < 3:

            @pl.when(s >= hop)
            def _():
                add_block(lax.rem(s - hop + NZ, NZ))

            @pl.when(s + hop >= NZ)
            def _():
                add_block(lax.rem(s + hop, NZ))

    for way in (0, 1):
        for piece in range(way * CUTS // 2, (way + 1) * CUTS // 2):
            zsends[way, 4, piece].wait_recv()
    last = [(lax.rem(s + NZ - 3, NZ), s >= 3), (lax.rem(s + 3, NZ), s + 3 >= NZ), (lax.rem(s + 4, NZ), s >= 4)]
    for k, (block, given) in enumerate(last):
        codes = vis[block]
        lhs[:, k * PAIR:(k + 1) * PAIR] = jnp.where(given, codes, jnp.zeros_like(codes))

    rs1 = {}
    for axis, q in PARTS:
        at = axis * HD + q * QW
        cols = slice(at, at + QW)
        rhs = jnp.concatenate([wd_s[block, :, cols] for block, _ in last], axis=0)
        part = acc[:, cols] + jnp.dot(lhs[...], rhs, preferred_element_type=F32)
        acc[:, cols] = part
        rb[:, :, :, cols] = part.astype(BF16).reshape(NX, NY, ROWS, QW)
        for o in (2, 1, 3):
            src = rb.at[o, :, :, columns(axis, q)] if axis == 0 else rb.at[:, o, :, columns(axis, q)]
            cp = remote(
                src, r1.at[axis, q, o - 1], c_ssem.at[0, q, axis, o - 1], c_rsem.at[0, q, axis, o - 1], along(axis, o)
            )
            cp.start()
            rs1[axis, q, o] = cp
    swap_c = remote(vis.at[:, :, pl.ds(FW, FW)], cs.at[:, 1], p_ssem.at[1], p_rsem.at[1], peer)
    swap_c.start()
    cs[:, 0] = vis[:, :, 0:FW]
    xt[:, 0:TOK] = xg[0].reshape(TOK, D).T
    small[3].wait()
    small[4].wait()
    rs2 = {}
    for axis, q in PARTS:
        at = axis * HD + q * QW
        cols = slice(at, at + QW)
        for o in (1, 3, 2):
            rs1[axis, q, o].wait_recv()
        for o in (2, 1, 3, 0):
            row = (o if axis == 0 else o * NY) * ROWS
            part = acc[row:row + ROWS, cols]
            for k in range(3):
                part = part + r1[axis, q, k, o].astype(F32)
            if o == 0:
                tot[:, cols] = part + bd_s[:, cols].astype(F32) - tg_s[:, cols].astype(F32)
            else:
                r2s[axis, q, o - 1] = part.astype(BF16)
                cp = remote(
                    r2s.at[axis, q, o - 1], r2.at[axis, q, o - 1],
                    c_ssem.at[1, q, axis, o - 1], c_rsem.at[1, q, axis, o - 1], along(1 - axis, o),
                )
                cp.start()
                rs2[axis, q, o] = cp

    ag_r1 = {}
    for axis, q in PARTS:
        at = axis * HD + q * QW
        cols = slice(at, at + QW)
        part = tot[:, cols]
        for o in (1, 3, 2):
            rs2[axis, q, o].wait_recv()
            part = part + r2[axis, q, o - 1].astype(F32)
        rg[0, 0, 0, :, cols] = part.astype(BF16)
        ag_r1[axis, q] = gather_first(axis, q, rg.at[0, 0, 0], rg, e_ssem, e_rsem, (0,))
        if axis == 1:
            for a in (0, 1):
                gather_first(a, q, rg.at[0, 0, 0], rg, e_ssem, e_rsem, (1,), ag_r1[a, q])
    ag_r = {p: gather_second_q(*p, ag_r1[p], rg, e_ssem, e_rsem) for p in PARTS}
    swap_x.wait_recv()
    xt[:, TOK:2 * TOK] = xg[1].reshape(TOK, D).T
    swap_c.wait_recv()
    for l in range(NZ):
        seen = cs[l].reshape(2 * TOK, FW).T
        ct[l] = jnp.where(s >= l, seen, jnp.zeros_like(seen))
    def grad_cols(block, at, width):
        return lax.dot_general(
            rg[0, :, :, :, at:at + width].reshape(TOK, width), wd_s[block, :, at:at + width],
            (((1,), (1,)), ((), ())), preferred_element_type=F32,
        )

    def grad_part(block, q):
        return grad_cols(block, q * QW, QW) + grad_cols(block, HD + q * QW, QW)

    def far(way, j):
        if way == 0:
            return lax.rem(s - j + NZ, NZ), s >= j
        return lax.rem(s + j, NZ), s + j >= NZ

    def gcopy(way, j, piece):
        return remote(
            zsb.at[way, j - 1, piece], zrb.at[way, j - 1, piece],
            g_ssem.at[way, j - 1, piece], g_rsem.at[way, j - 1, piece], ((down, down2), (up, up2))[way][j == 4],
        )

    gsends = {}

    def pass_on(way, j, piece, slot, given):
        part = jnp.where(given, acc[piece * PIECE:(piece + 1) * PIECE, slot * PAIR:(slot + 1) * PAIR], 0.0)
        for k in {2: (4, 3) if piece * 2 // CUTS == way else (3,), 1: (2,)}.get(j, ()):
            gsends[way, k, piece].wait_recv()
            part = part + zrb[way, k - 1, piece].astype(F32)
        zsb[way, j - 1, piece] = part.astype(BF16)
        cp = gcopy(way, j, piece)
        cp.start()
        gsends[way, j, piece] = cp

    gather_end_q(0, ag_r1, ag_r)
    for way in (0, 1):
        acc[:, way * PAIR:(way + 1) * PAIR] = grad_part(far(way, 3)[0], 0)
    gather_end_q(1, ag_r1, ag_r)
    for way in (0, 1):
        acc[:, way * PAIR:(way + 1) * PAIR] += grad_part(far(way, 3)[0], 1)
        for piece in range(CUTS):
            pass_on(way, 3, piece, way, far(way, 3)[1])
    acc[:, 0:PAIR] = grad_cols(far(0, 4)[0], 0, D)
    for piece in range(CUTS):
        pass_on(piece * 2 // CUTS, 4, piece, 0, far(0, 4)[1])
    swap_r = remote(rg.at[0], rg.at[1], p_ssem.at[2], p_rsem.at[2], peer)
    swap_r.start()

    def dec_tile(j):
        col = slice(j * TILE, (j + 1) * TILE)
        part = jnp.dot(
            ct[...].reshape(NZ * FW, 2 * TOK), rg[...].reshape(2 * TOK, D)[:, col], preferred_element_type=F32
        )
        dg_ref[:, :, col] = part.astype(BF16).reshape(NZ, FW, TILE)

    for j in (2, 1):
        for way in (0, 1):
            acc[:, way * PAIR:(way + 1) * PAIR] = grad_cols(far(way, j)[0], 0, D)
        if j == 1:
            swap_r.wait_recv()
            dec_tile(0)
        for piece in range(CUTS):
            for way in (0, 1):
                pass_on(way, j, piece, way, far(way, j)[1])

    acc[:, 0:PAIR] = grad_cols(s, 0, D)
    for j in range(1, D // TILE):
        dec_tile(j)
    for piece in range(CUTS):
        rows = slice(piece * PIECE, (piece + 1) * PIECE)
        own = acc[rows, 0:PAIR]
        for way in (0, 1):
            gsends[way, 1, piece].wait_recv()
            own = own + zrb[way, 0, piece].astype(F32)
        grad = (own * live[rows, :]).astype(BF16)
        pg_s[0, 0, rows, :] = grad[:, 0:FW]
        pg_s[1, 0, rows, :] = grad[:, FW:PAIR]
    swap_g = remote(pg_s.at[1, 0], pg_s.at[0, 1], p_ssem.at[3], p_rsem.at[3], peer)
    swap_g.start()
    own = jnp.dot(xt[:, 0:TOK], pg_s[0, 0], preferred_element_type=F32)
    swap_g.wait_recv()
    eg_ref[...] = (own + jnp.dot(xt[:, TOK:2 * TOK], pg_s[0, 1], preferred_element_type=F32)).astype(BF16)
    bg_ref[...] = jnp.sum(pg_s[0].reshape(2 * TOK, FW).astype(F32), axis=0, keepdims=True)

    for first in list(ag_x1.values()) + list(ag_r1.values()):
        for cp in first.values():
            cp.wait_send()
    for cp in list(rs1.values()) + list(rs2.values()):
        cp.wait_send()
    for copies in ag_x:
        for cp in copies.values():
            cp.wait_send()
    for copies in ag_r.values():
        for cp in copies:
            cp.wait_send()
    for cp in swap + [swap_x, swap_c, swap_r, swap_g]:
        cp.wait_send()
    for cp in list(zsends.values()) + list(gsends.values()):
        cp.wait_send()


def fused(x, we, be, wd, bd, tg, act):
    vmem = pl.BlockSpec(memory_space=pltpu.VMEM)
    hbm = pl.BlockSpec(memory_space=pl.ANY)
    dma = pltpu.SemaphoreType.DMA
    return pl.pallas_call(
        step_kernel,
        name="step",
        out_shape=(
            pltpu.VMEM((D, FW), BF16),
            pltpu.VMEM((1, FW), F32),
            pltpu.VMEM((NZ, FW, D), BF16),
        ),
        in_specs=[pl.BlockSpec(memory_space=pltpu.HBM)] * 7,
        out_specs=(vmem, vmem, vmem),
        scratch_shapes=[
            pltpu.VMEM((2, NX, NY, ROWS, D), BF16),
            pltpu.VMEM((2, NX, NY, ROWS, D), BF16),
            pltpu.VMEM((D, PAIR), BF16),
            pltpu.VMEM((NZ, PAIR, D), BF16),
            pltpu.VMEM((2, 1, FW), F32),
            pltpu.VMEM((1, D), BF16),
            pltpu.VMEM((ROWS, D), BF16),
            pltpu.VMEM((8, CHIPS), jnp.int32),
            pltpu.VMEM((NZ, TOK, PAIR), BF16),
            pltpu.VMEM((TOK, PAIR), F32),
            pltpu.VMEM((TOK, D), F32),
            pltpu.VMEM((NX, NY, ROWS, D), BF16),
            pltpu.VMEM((2, 2, 3, 4, ROWS, QW), BF16),
            pltpu.VMEM((2, 2, 3, ROWS, QW), BF16),
            pltpu.VMEM((2, 2, 3, ROWS, QW), BF16),
            pltpu.VMEM((TOK, 3 * PAIR), BF16),
            pltpu.VMEM((ROWS, D), F32),
            pltpu.VMEM((NZ, 2, TOK, FW), BF16),
            pltpu.VMEM((NZ, FW, 2 * TOK), BF16),
            pltpu.VMEM((D, 2 * TOK), BF16),
            pltpu.VMEM((2, 2, TOK, FW), BF16),
            pltpu.VMEM((2, 4, CUTS, PIECE, PAIR), BF16),
            pltpu.VMEM((2, 4, CUTS, PIECE, PAIR), BF16),
            dma((NZ + 1,)), dma((NZ + 2,)), dma((NZ + 2,)),
            dma((2, 2, 2, 3)), dma((2, 2, 2, 3)),
            dma((2, 2, 6)), dma((2, 2, 6)),
            dma((2, 4, CUTS)), dma((2, 4, CUTS)),
            dma((2, 2, 2, 3)), dma((2, 2, 2, 3)),
            dma((3, 2, 2, 3)), dma((3, 2, 2, 3)),
            dma((2, 4, CUTS)), dma((2, 4, CUTS)),
            dma((4,)), dma((4,)),
            dma((5,)),
        ],
        compiler_params=pltpu.CompilerParams(
            collective_id=0, has_side_effects=True, vmem_limit_bytes=44 * 2**20
        ),
    )(x, we, be, wd, bd, tg, act)


def store_kernel(e_ref, b_ref, d_ref, eo_ref, bo_ref, do_ref, sem):
    copies = [pltpu.make_async_copy(e_ref, eo_ref, sem.at[0]), pltpu.make_async_copy(b_ref, bo_ref, sem.at[1])]
    copies += [pltpu.make_async_copy(d_ref.at[l], do_ref.at[l], sem.at[2 + l]) for l in range(NZ)]
    for cp in copies:
        cp.start()
    for cp in copies:
        cp.wait()


def store(e, b, d):
    hbm = pl.BlockSpec(memory_space=pl.ANY)
    return pl.pallas_call(
        store_kernel,
        name="store",
        out_shape=tuple(jax.ShapeDtypeStruct(a.shape, a.dtype) for a in (e, b, d)),
        in_specs=[hbm] * 3,
        out_specs=(hbm,) * 3,
        scratch_shapes=[pltpu.SemaphoreType.DMA((2 + NZ,))],
        compiler_params=pltpu.CompilerParams(vmem_limit_bytes=2**20),
    )(e, b, d)


def body(inputs, enc_weight, enc_bias, dec_weight, dec_bias, target, active):
    args = (inputs[0], enc_weight[0], enc_bias, dec_weight[0], dec_bias, target[0], active[0].T)
    enc_grad, bias_grad, dec_grad = fused(*(pltpu.with_memory_space_constraint(a, pltpu.HBM) for a in args))
    enc_grad, bias_grad, dec_grad = store(enc_grad, bias_grad, dec_grad)
    return enc_grad[None], bias_grad, dec_grad[None]


def solution(mesh):
    return jax.shard_map(
        body,
        mesh=mesh,
        in_specs=(
            P("section", "feat", None),
            P("section", None, "feat"),
            P("section", "feat"),
            P("section", None, "feat", None),
            P("section", None),
            P("section", "feat", None),
            P("section", None, None),
        ),
        out_specs=(
            P("section", None, "feat"),
            P("section", "feat"),
            P("section", None, "feat", None),
        ),
        check_vma=False,
    )
```

```python
import functools

import jax
import jax.numpy as jnp
from jax import lax
from jax.experimental import pallas as pl
from jax.experimental.pallas import tpu as pltpu
from jax.sharding import PartitionSpec as P

MESH = pl.DeviceIdType.MESH
BF16 = jnp.bfloat16
F32 = jnp.float32

NX = 4
NY = 4
CHIPS = NX * NY
NZ = 8
ROWS = 16
FW = 128
D = 2560
TOK = CHIPS * ROWS
PAIR = 2 * FW
CUTS = 4
PIECE = TOK // CUTS
TILE = 512

HD = D // 2
QW = HD // 2
PARTS = [(axis, q) for q in (0, 1) for axis in (0, 1)]


def step_kernel(
    x_ref, we_ref, be_ref, wd_ref, bd_ref, tg_ref, act_ref,
    eg_ref, bg_ref, dg_ref,
    xg, rg, we_s, wd_s, be_s, bd_s, tg_s, act_s, vis, live, acc, rb, r1, r2s, r2, lhs, tot, cs, ct, xt, pg_s, zsb, zrb,
    in_sem, in_ssem, in_rsem, a_ssem, a_rsem, a2_ssem, a2_rsem, b_ssem, b_rsem, c_ssem, c_rsem,
    e_ssem, e_rsem, g_ssem, g_rsem, p_ssem, p_rsem, small_sem,
):
    s = lax.axis_index("section")
    f = lax.axis_index("feat")
    core = lax.rem(f, 2)
    chip = lax.div(f, 2)
    cx = lax.div(chip, NY)
    cy = lax.rem(chip, NY)

    def along(axis, step):
        x = lax.rem(cx + step, NX) if axis == 0 else cx
        y = lax.rem(cy + step, NY) if axis == 1 else cy
        return {"section": s, "feat": (x * NY + y) * 2 + core}

    peer = {"section": s, "feat": chip * 2 + 1 - core}
    up = {"section": lax.rem(s + 1, NZ), "feat": f}
    down = {"section": lax.rem(s + NZ - 1, NZ), "feat": f}
    up2 = {"section": lax.rem(s + 2, NZ), "feat": f}
    down2 = {"section": lax.rem(s + NZ - 2, NZ), "feat": f}

    def remote(src, dst, ssem, rsem, dev):
        return pltpu.make_async_remote_copy(
            src_ref=src, dst_ref=dst, send_sem=ssem, recv_sem=rsem, device_id=dev, device_id_type=MESH
        )

    barrier = pltpu.get_barrier_semaphore()
    for dev in [peer, up, down, up2, down2] + [along(axis, o) for axis in (0, 1) for o in (1, 2, 3)]:
        pl.semaphore_signal(barrier, inc=1, device_id=dev, device_id_type=MESH)

    loc = [pltpu.make_async_copy(we_ref, we_s.at[:, pl.ds(0, FW)], in_sem.at[NZ])]
    for l in range(NZ):
        loc.append(pltpu.make_async_copy(wd_ref.at[l], wd_s.at[l, pl.ds(0, FW)], in_sem.at[l]))
    small = [
        pltpu.make_async_copy(a, b, small_sem.at[k])
        for k, (a, b) in enumerate(
            [(act_ref, act_s), (be_ref, be_s.at[0]), (x_ref, xg.at[0, 0, 0]), (bd_ref, bd_s), (tg_ref, tg_s)]
        )
    ]
    for cp in small + loc:
        cp.start()

    pl.semaphore_wait(barrier, 11)

    def columns(axis, q):
        return pl.ds(axis * HD + q * QW, QW)

    def gather_first(axis, q, src, g, ssem, rsem, turns=(0, 1), copies=None):
        copies = {} if copies is None else copies
        for turn in turns:
            way = axis if turn == 0 else 1 - axis
            for o in (2, 1, 3):
                there = (NX - o, 0) if way == 0 else (0, NY - o)
                cols = columns(axis, q)
                cp = remote(
                    src.at[:, cols], g.at[0, there[0], there[1], :, cols],
                    ssem.at[turn, q, axis, o - 1], rsem.at[turn, q, axis, o - 1], along(way, o),
                )
                cp.start()
                copies[turn, o] = cp
        return copies

    def gather_second(half, first, g, ssem, rsem):
        copies = {}
        for axis, q in [(a, b) for b in (0, 1) for a in (0, 1)]:
            cols = columns(axis, q)
            if axis == 0:
                for o in ((3,), (1, 2))[half]:
                    first[axis, q][0, o].wait_recv()
                at, count = ((1, 1), (2, 2))[half]
                for o in (2, 1, 3):
                    src, dst = g.at[0, pl.ds(at, count), 0, :, cols], g.at[0, pl.ds(at, count), NY - o, :, cols]
                    k = half * 3 + o - 1
                    copies[axis, q, o] = remote(src, dst, ssem.at[q, axis, k], rsem.at[q, axis, k], along(1, o))
                    copies[axis, q, o].start()
            else:
                if half == 0:
                    for o in (1, 3, 2):
                        first[axis, q][0, o].wait_recv()
                for o in ((3,), (2, 1))[half]:
                    src, dst = g.at[0, 0, pl.ds(1, 3), :, cols], g.at[0, NX - o, pl.ds(1, 3), :, cols]
                    copies[axis, q, o] = remote(src, dst, ssem.at[q, axis, o - 1], rsem.at[q, axis, o - 1], along(0, o))
                    copies[axis, q, o].start()
        return copies

    def gather_end(half, first, second):
        for q in (0, 1):
            if half == 0:
                for o in (1, 3, 2):
                    first[0, q][1, o].wait_recv()
            for o in ((3,), (1, 2))[half]:
                first[1, q][1, o].wait_recv()
        for cp in second[half].values():
            cp.wait_recv()

    def gather_second_q(axis, q, first, g, ssem, rsem):
        copies = []
        for o in (1, 3, 2):
            first[0, o].wait_recv()
        for o in (2, 1, 3):
            cols = columns(axis, q)
            if axis == 0:
                src, dst = g.at[0, pl.ds(1, 3), 0, :, cols], g.at[0, pl.ds(1, 3), NY - o, :, cols]
            else:
                src, dst = g.at[0, 0, pl.ds(1, 3), :, cols], g.at[0, NX - o, pl.ds(1, 3), :, cols]
            cp = remote(src, dst, ssem.at[2, q, axis, o - 1], rsem.at[2, q, axis, o - 1], along(1 - axis, o))
            cp.start()
            copies.append(cp)
        return copies

    def gather_end_q(q, first, second):
        for axis in (0, 1):
            for o in (1, 3, 2):
                first[axis, q][1, o].wait_recv()
            for cp in second[axis, q]:
                cp.wait_recv()

    ag_x1 = {p: gather_first(*p, x_ref, xg, a_ssem, a_rsem, (0,)) for p in PARTS}
    for p in PARTS:
        gather_first(*p, x_ref, xg, a_ssem, a_rsem, (1,), ag_x1[p])
    swap = [
        remote(we_ref, we_s.at[:, pl.ds(FW, FW)], in_ssem.at[NZ], in_rsem.at[NZ], peer),
        remote(be_ref, be_s.at[1], in_ssem.at[NZ + 1], in_rsem.at[NZ + 1], peer),
    ]
    for l in range(NZ):
        swap.append(remote(wd_ref.at[l], wd_s.at[l, pl.ds(FW, FW)], in_ssem.at[l], in_rsem.at[l], peer))
    for cp in swap:
        cp.start()

    small[0].wait()
    act = act_s[...]
    row_at = lax.broadcasted_iota(jnp.int32, (TOK, CHIPS), 0) // ROWS
    row_chip = lax.rem(cx + row_at // NY, NX) * NY + lax.rem(cy + lax.rem(row_at, NY), NY)
    expand = (row_chip == lax.broadcasted_iota(jnp.int32, (TOK, CHIPS), 1)).astype(F32)

    def keep_of(block):
        hit = jnp.max((act == block).astype(F32), axis=0, keepdims=True)
        return jnp.broadcast_to(jnp.sum(expand * hit, axis=1, keepdims=True), (TOK, FW))

    live[:, 0:FW] = keep_of(f)
    live[:, FW:PAIR] = keep_of(chip * 2 + 1 - core)

    ag_x = [gather_second(half, ag_x1, xg, a2_ssem, a2_rsem) for half in (0, 1)]
    small[1].wait()
    small[2].wait()
    loc[0].wait()
    swap[0].wait_recv()
    swap[1].wait_recv()
    def zcopy(way, hop, piece):
        held = 2 if hop == 4 else hop - 1
        block = lax.rem(s - held + NZ, NZ) if way == 0 else lax.rem(s + held, NZ)
        ref = vis.at[block, pl.ds(piece * PIECE, PIECE)]
        dev = ((up, up2), (down, down2))[way][hop == 4]
        return remote(ref, ref, b_ssem.at[way, hop - 1, piece], b_rsem.at[way, hop - 1, piece], dev)

    zsends = {}
    bias = jnp.concatenate([be_s[0], be_s[1]], axis=1)
    for half in (0, 1):
        gather_end(half, ag_x1, ag_x)
        rows = slice(half * TOK // 2, (half + 1) * TOK // 2)
        x = xg[0, half * NX // 2:(half + 1) * NX // 2].reshape(TOK // 2, D)
        pre = jnp.dot(x, we_s[...], preferred_element_type=F32) + bias
        mask = live[rows, :] * (pre > 0).astype(F32)
        live[rows, :] = mask
        vis[s, rows, :] = (mask * pre).astype(BF16)
        for piece in range(half * CUTS // 2, (half + 1) * CUTS // 2):
            for way in (0, 1):
                cp = zcopy(way, 1, piece)
                cp.start()
                zsends[way, 1, piece] = cp

    swap_x = remote(xg.at[0], xg.at[1], p_ssem.at[0], p_rsem.at[0], peer)
    swap_x.start()

    for l in range(NZ):
        loc[1 + l].wait()
        swap[2 + l].wait_recv()

    def add_block(block, first=False):
        @pl.loop(0, D // TILE)
        def _(j):
            col = pl.ds(pl.multiple_of(j * TILE, TILE), TILE)
            part = jnp.dot(vis[block], wd_s[block, :, col], preferred_element_type=F32)
            if first:
                acc[:, col] = part
            else:
                acc[:, col] += part

    add_block(s, True)
    for hop in (1, 2, 3):
        for piece in range(CUTS):
            for way in (0, 1):
                zsends[way, hop, piece].wait_recv()
                for later in ((2,), (4, 3) if piece * 2 // CUTS == way else (3,), ())[hop - 1]:
                    cp = zcopy(way, later, piece)
                    cp.start()
                    zsends[way, later, piece] = cp

        if hop < 3:

            @pl.when(s >= hop)
            def _():
                add_block(lax.rem(s - hop + NZ, NZ))

            @pl.when(s + hop >= NZ)
            def _():
                add_block(lax.rem(s + hop, NZ))

    for way in (0, 1):
        for piece in range(way * CUTS // 2, (way + 1) * CUTS // 2):
            zsends[way, 4, piece].wait_recv()
    last = [(lax.rem(s + NZ - 3, NZ), s >= 3), (lax.rem(s + 3, NZ), s + 3 >= NZ), (lax.rem(s + 4, NZ), s >= 4)]
    for k, (block, given) in enumerate(last):
        codes = vis[block]
        lhs[:, k * PAIR:(k + 1) * PAIR] = jnp.where(given, codes, jnp.zeros_like(codes))

    rs1 = {}
    for axis, q in PARTS:
        at = axis * HD + q * QW
        cols = slice(at, at + QW)
        rhs = jnp.concatenate([wd_s[block, :, cols] for block, _ in last], axis=0)
        part = acc[:, cols] + jnp.dot(lhs[...], rhs, preferred_element_type=F32)
        acc[:, cols] = part
        rb[:, :, :, cols] = part.astype(BF16).reshape(NX, NY, ROWS, QW)
        for o in (2, 1, 3):
            src = rb.at[o, :, :, columns(axis, q)] if axis == 0 else rb.at[:, o, :, columns(axis, q)]
            cp = remote(
                src, r1.at[axis, q, o - 1], c_ssem.at[0, q, axis, o - 1], c_rsem.at[0, q, axis, o - 1], along(axis, o)
            )
            cp.start()
            rs1[axis, q, o] = cp
    swap_c = remote(vis.at[:, :, pl.ds(FW, FW)], cs.at[:, 1], p_ssem.at[1], p_rsem.at[1], peer)
    swap_c.start()
    cs[:, 0] = vis[:, :, 0:FW]
    xt[:, 0:TOK] = xg[0].reshape(TOK, D).T
    small[3].wait()
    small[4].wait()
    rs2 = {}
    for axis, q in PARTS:
        at = axis * HD + q * QW
        cols = slice(at, at + QW)
        for o in (1, 3, 2):
            rs1[axis, q, o].wait_recv()
        for o in (2, 1, 3, 0):
            row = (o if axis == 0 else o * NY) * ROWS
            part = acc[row:row + ROWS, cols]
            for k in range(3):
                part = part + r1[axis, q, k, o].astype(F32)
            if o == 0:
                tot[:, cols] = part + bd_s[:, cols].astype(F32) - tg_s[:, cols].astype(F32)
            else:
                r2s[axis, q, o - 1] = part.astype(BF16)
                cp = remote(
                    r2s.at[axis, q, o - 1], r2.at[axis, q, o - 1],
                    c_ssem.at[1, q, axis, o - 1], c_rsem.at[1, q, axis, o - 1], along(1 - axis, o),
                )
                cp.start()
                rs2[axis, q, o] = cp

    ag_r1 = {}
    for axis, q in PARTS:
        at = axis * HD + q * QW
        cols = slice(at, at + QW)
        part = tot[:, cols]
        for o in (1, 3, 2):
            rs2[axis, q, o].wait_recv()
            part = part + r2[axis, q, o - 1].astype(F32)
        rg[0, 0, 0, :, cols] = part.astype(BF16)
        ag_r1[axis, q] = gather_first(axis, q, rg.at[0, 0, 0], rg, e_ssem, e_rsem, (0,))
        if axis == 1:
            for a in (0, 1):
                gather_first(a, q, rg.at[0, 0, 0], rg, e_ssem, e_rsem, (1,), ag_r1[a, q])
    ag_r = {p: gather_second_q(*p, ag_r1[p], rg, e_ssem, e_rsem) for p in PARTS}
    swap_x.wait_recv()
    xt[:, TOK:2 * TOK] = xg[1].reshape(TOK, D).T
    swap_c.wait_recv()
    for l in range(NZ):
        seen = cs[l].reshape(2 * TOK, FW).T
        ct[l] = jnp.where(s >= l, seen, jnp.zeros_like(seen))
    def grad_cols(block, at, width):
        return lax.dot_general(
            rg[0, :, :, :, at:at + width].reshape(TOK, width), wd_s[block, :, at:at + width],
            (((1,), (1,)), ((), ())), preferred_element_type=F32,
        )

    def grad_part(block, q):
        return grad_cols(block, q * QW, QW) + grad_cols(block, HD + q * QW, QW)

    def far(way, j):
        if way == 0:
            return lax.rem(s - j + NZ, NZ), s >= j
        return lax.rem(s + j, NZ), s + j >= NZ

    def gcopy(way, j, piece):
        return remote(
            zsb.at[way, j - 1, piece], zrb.at[way, j - 1, piece],
            g_ssem.at[way, j - 1, piece], g_rsem.at[way, j - 1, piece], ((down, down2), (up, up2))[way][j == 4],
        )

    gsends = {}

    def pass_on(way, j, piece, slot, given):
        part = jnp.where(given, acc[piece * PIECE:(piece + 1) * PIECE, slot * PAIR:(slot + 1) * PAIR], 0.0)
        for k in {2: (4, 3) if piece * 2 // CUTS == way else (3,), 1: (2,)}.get(j, ()):
            gsends[way, k, piece].wait_recv()
            part = part + zrb[way, k - 1, piece].astype(F32)
        zsb[way, j - 1, piece] = part.astype(BF16)
        cp = gcopy(way, j, piece)
        cp.start()
        gsends[way, j, piece] = cp

    gather_end_q(0, ag_r1, ag_r)
    for way in (0, 1):
        acc[:, way * PAIR:(way + 1) * PAIR] = grad_part(far(way, 3)[0], 0)
    gather_end_q(1, ag_r1, ag_r)
    for way in (0, 1):
        acc[:, way * PAIR:(way + 1) * PAIR] += grad_part(far(way, 3)[0], 1)
        for piece in range(CUTS):
            pass_on(way, 3, piece, way, far(way, 3)[1])
    acc[:, 0:PAIR] = grad_cols(far(0, 4)[0], 0, D)
    for piece in range(CUTS):
        pass_on(piece * 2 // CUTS, 4, piece, 0, far(0, 4)[1])
    swap_r = remote(rg.at[0], rg.at[1], p_ssem.at[2], p_rsem.at[2], peer)
    swap_r.start()

    def dec_tile(j):
        col = slice(j * TILE, (j + 1) * TILE)
        part = jnp.dot(
            ct[...].reshape(NZ * FW, 2 * TOK), rg[...].reshape(2 * TOK, D)[:, col], preferred_element_type=F32
        )
        dg_ref[:, :, col] = part.astype(BF16).reshape(NZ, FW, TILE)

    for j in (2, 1):
        for way in (0, 1):
            acc[:, way * PAIR:(way + 1) * PAIR] = grad_cols(far(way, j)[0], 0, D)
        if j == 1:
            swap_r.wait_recv()
            dec_tile(0)
        for piece in range(CUTS):
            for way in (0, 1):
                pass_on(way, j, piece, way, far(way, j)[1])

    acc[:, 0:PAIR] = grad_cols(s, 0, D)
    for j in range(1, D // TILE):
        dec_tile(j)
    swap_g = []
    for piece in range(CUTS):
        rows = slice(piece * PIECE, (piece + 1) * PIECE)
        own = acc[rows, 0:PAIR]
        for way in (0, 1):
            gsends[way, 1, piece].wait_recv()
            own = own + zrb[way, 0, piece].astype(F32)
        grad = (own * live[rows, :]).astype(BF16)
        pg_s[0, 0, rows, :] = grad[:, 0:FW]
        pg_s[1, 0, rows, :] = grad[:, FW:PAIR]
        if piece % 2 == 1:
            part = pl.ds((piece - 1) * PIECE, 2 * PIECE)
            k = 3 + piece // 2
            swap_g.append(remote(pg_s.at[1, 0, part], pg_s.at[0, 1, part], p_ssem.at[k], p_rsem.at[k], peer))
            swap_g[-1].start()
    own = jnp.dot(xt[:, 0:TOK], pg_s[0, 0], preferred_element_type=F32)
    for cp in swap_g:
        cp.wait_recv()
    eg_ref[...] = (own + jnp.dot(xt[:, TOK:2 * TOK], pg_s[0, 1], preferred_element_type=F32)).astype(BF16)
    bg_ref[...] = jnp.sum(pg_s[0].reshape(2 * TOK, FW).astype(F32), axis=0, keepdims=True)

    for first in list(ag_x1.values()) + list(ag_r1.values()):
        for cp in first.values():
            cp.wait_send()
    for cp in list(rs1.values()) + list(rs2.values()):
        cp.wait_send()
    for copies in ag_x:
        for cp in copies.values():
            cp.wait_send()
    for copies in ag_r.values():
        for cp in copies:
            cp.wait_send()
    for cp in swap + [swap_x, swap_c, swap_r] + swap_g:
        cp.wait_send()
    for cp in list(zsends.values()) + list(gsends.values()):
        cp.wait_send()


def fused(x, we, be, wd, bd, tg, act):
    vmem = pl.BlockSpec(memory_space=pltpu.VMEM)
    hbm = pl.BlockSpec(memory_space=pl.ANY)
    dma = pltpu.SemaphoreType.DMA
    return pl.pallas_call(
        step_kernel,
        name="step",
        out_shape=(
            pltpu.VMEM((D, FW), BF16),
            pltpu.VMEM((1, FW), F32),
            pltpu.VMEM((NZ, FW, D), BF16),
        ),
        in_specs=[pl.BlockSpec(memory_space=pltpu.HBM)] * 7,
        out_specs=(vmem, vmem, vmem),
        scratch_shapes=[
            pltpu.VMEM((2, NX, NY, ROWS, D), BF16),
            pltpu.VMEM((2, NX, NY, ROWS, D), BF16),
            pltpu.VMEM((D, PAIR), BF16),
            pltpu.VMEM((NZ, PAIR, D), BF16),
            pltpu.VMEM((2, 1, FW), F32),
            pltpu.VMEM((1, D), BF16),
            pltpu.VMEM((ROWS, D), BF16),
            pltpu.VMEM((8, CHIPS), jnp.int32),
            pltpu.VMEM((NZ, TOK, PAIR), BF16),
            pltpu.VMEM((TOK, PAIR), F32),
            pltpu.VMEM((TOK, D), F32),
            pltpu.VMEM((NX, NY, ROWS, D), BF16),
            pltpu.VMEM((2, 2, 3, 4, ROWS, QW), BF16),
            pltpu.VMEM((2, 2, 3, ROWS, QW), BF16),
            pltpu.VMEM((2, 2, 3, ROWS, QW), BF16),
            pltpu.VMEM((TOK, 3 * PAIR), BF16),
            pltpu.VMEM((ROWS, D), F32),
            pltpu.VMEM((NZ, 2, TOK, FW), BF16),
            pltpu.VMEM((NZ, FW, 2 * TOK), BF16),
            pltpu.VMEM((D, 2 * TOK), BF16),
            pltpu.VMEM((2, 2, TOK, FW), BF16),
            pltpu.VMEM((2, 4, CUTS, PIECE, PAIR), BF16),
            pltpu.VMEM((2, 4, CUTS, PIECE, PAIR), BF16),
            dma((NZ + 1,)), dma((NZ + 2,)), dma((NZ + 2,)),
            dma((2, 2, 2, 3)), dma((2, 2, 2, 3)),
            dma((2, 2, 6)), dma((2, 2, 6)),
            dma((2, 4, CUTS)), dma((2, 4, CUTS)),
            dma((2, 2, 2, 3)), dma((2, 2, 2, 3)),
            dma((3, 2, 2, 3)), dma((3, 2, 2, 3)),
            dma((2, 4, CUTS)), dma((2, 4, CUTS)),
            dma((5,)), dma((5,)),
            dma((5,)),
        ],
        compiler_params=pltpu.CompilerParams(
            collective_id=0, has_side_effects=True, vmem_limit_bytes=44 * 2**20
        ),
    )(x, we, be, wd, bd, tg, act)


def store_kernel(e_ref, b_ref, d_ref, eo_ref, bo_ref, do_ref, sem):
    copies = [pltpu.make_async_copy(e_ref, eo_ref, sem.at[0]), pltpu.make_async_copy(b_ref, bo_ref, sem.at[1])]
    copies += [pltpu.make_async_copy(d_ref.at[l], do_ref.at[l], sem.at[2 + l]) for l in range(NZ)]
    for cp in copies:
        cp.start()
    for cp in copies:
        cp.wait()


def store(e, b, d):
    hbm = pl.BlockSpec(memory_space=pl.ANY)
    return pl.pallas_call(
        store_kernel,
        name="store",
        out_shape=tuple(jax.ShapeDtypeStruct(a.shape, a.dtype) for a in (e, b, d)),
        in_specs=[hbm] * 3,
        out_specs=(hbm,) * 3,
        scratch_shapes=[pltpu.SemaphoreType.DMA((2 + NZ,))],
        compiler_params=pltpu.CompilerParams(vmem_limit_bytes=2**20),
    )(e, b, d)


def body(inputs, enc_weight, enc_bias, dec_weight, dec_bias, target, active):
    args = (inputs[0], enc_weight[0], enc_bias, dec_weight[0], dec_bias, target[0], active[0].T)
    enc_grad, bias_grad, dec_grad = fused(*(pltpu.with_memory_space_constraint(a, pltpu.HBM) for a in args))
    enc_grad, bias_grad, dec_grad = store(enc_grad, bias_grad, dec_grad)
    return enc_grad[None], bias_grad, dec_grad[None]


def solution(mesh):
    return jax.shard_map(
        body,
        mesh=mesh,
        in_specs=(
            P("section", "feat", None),
            P("section", None, "feat"),
            P("section", "feat"),
            P("section", None, "feat", None),
            P("section", None),
            P("section", "feat", None),
            P("section", None, None),
        ),
        out_specs=(
            P("section", None, "feat"),
            P("section", "feat"),
            P("section", None, "feat", None),
        ),
        check_vma=False,
    )
```
